32 devices in a mesh: row: 4 (over y, x), col: 8 (over z, core).
Axes of the slice: x: 2, y: 2, z: 4, core: 2. Of those that a mesh axis runs over, the one named last changes fastest.
Arguments:
- grad_out: bfloat16 [4096, 8192], P('col', 'row'), may hold values from -4 to 4
- proj_weight: bfloat16 [8192, 4096], P('col', 'row'), may hold values from -0.09375 to 0.09375
- queries: bfloat16 [4096, 4096], P('col', 'row'), may hold values from -5 to 5
- keys: bfloat16 [4096, 4096], P('col', 'row'), may hold values from -5 to 5
- values: bfloat16 [4096, 4096], P('col', 'row'), may hold values from -6 to 6
- cache_keys: bfloat16 [1024, 4096], P('col', 'row'), may hold values from -6 to 6
- cache_values: bfloat16 [1024, 4096], P('col', 'row'), may hold values from -6 to 6
- block_table: int32 [32, 4], P('col'), may hold values from 0 to 7, all different within a row
Outputs:
- grad_q: bfloat16 [4096, 4096], P('col', 'row')
- grad_k: bfloat16 [4096, 4096], P('col', 'row')
- grad_v: bfloat16 [4096, 4096], P('col', 'row')
- grad_cache_k: float32 [1024, 4096], P('col', 'row')
- grad_cache_v: float32 [1024, 4096], P('col', 'row')
- grad_weight: bfloat16 [8192, 4096], P('col', 'row')
The draws below stay inside these ranges and needn't reach their ends.
Inputs may be any that keep to these rules, and one draw needn't show every extreme that they name: `block_table`: each row names 4 different cached blocks, and every cached block is named by some row.
All inputs are finite; a program needn't handle non-finite values.
Results may differ from the reference program's by a relative error of at most 0.023.
Values may be sent and summed in bfloat16 or wider, within the bound.
A program may use at most 128 MiB of HBM per device.

```python
import math
import jax
import jax.numpy as jnp
from jax import lax

D = 8192
HEADS = 32
HEAD_DIM = 128
BLOCK = 128
CB = 8
KB = 4
TOKENS = 4096
CACHE = 1024
QBLOCKS = 32
N_COL = 8


def normal_field(first_key, second_key, spread):
    entries = jax.random.normal(first_key, (TOKENS, HEADS * HEAD_DIM), jnp.float32)
    row_scale = jnp.exp(jax.random.uniform(second_key, (TOKENS, 1), jnp.float32, -spread, spread))
    return jnp.clip(entries * row_scale, -5.0, 5.0)


def draw_queries(key, part):
    key = jax.random.fold_in(key, 1)
    first_key, second_key = jax.random.split(key)
    return normal_field(first_key, second_key, 0.8).astype(jnp.bfloat16)


def draw_keys(key, part):
    key = jax.random.fold_in(key, 2)
    first_key, second_key = jax.random.split(key)
    return normal_field(first_key, second_key, 0.8).astype(jnp.bfloat16)


def raised(values, stream_key, source, target, blocks, factor):
    owner, partner = [(jnp.arange(values.shape[dim]) // (values.shape[dim] // blocks)).reshape([-1 if axis == dim else 1 for axis in range(values.ndim)]) for dim in (source, target)]
    chosen = jax.random.permutation(stream_key, blocks)[partner]
    strong = (owner == chosen) | (owner == (partner + blocks // 2) % blocks)
    return jnp.where(strong, factor * values, values)


def steps_of(key, extent, pieces, smallest, top_value):
    level, own = 1.0, jax.random.fold_in(key, 6)
    for dim, parts in pieces:
        draws = jnp.exp(jax.random.uniform(jax.random.fold_in(own, dim), (parts,), jnp.float32, smallest / len(pieces), top_value / len(pieces)))
        level = level * jnp.repeat(draws, extent[dim] // parts).reshape([-1 if axis == dim else 1 for axis in range(len(extent))])
    return level


def different_ones(own_key, rows, amount, top, lift):
    order = jax.random.permutation(jax.random.fold_in(own_key, 1), amount)
    favour = order
    for power in range(3):
        favour = favour * favour // amount
    favour = favour * lift // amount
    chance = jax.random.randint(jax.random.fold_in(own_key, 2), (rows, amount), 0, 4096) + favour
    sure = jax.random.permutation(jax.random.fold_in(own_key, 3), rows)[jnp.arange(amount) % rows]
    chance = jnp.where(jnp.arange(rows)[:, None] == sure[None, :], 1 << 14, chance)
    score = chance * amount + jnp.arange(amount)
    return lax.top_k(score.astype(jnp.int32), top)[1].astype(jnp.int32)


def noise(own_key, dims, scale, bound, shards=(), held_as=jnp.bfloat16):
    result = scale * jax.random.normal(own_key, dims, jnp.float32)
    if shards:
        result = result * steps_of(own_key, dims, shards, -0.22, 0.18)
    return jnp.clip(result, -bound, bound).astype(held_as)


def bell_draw_with(key, extent, deviation, bound, shards, heavy, held_as=jnp.bfloat16):
    result = deviation * jax.random.normal(key, extent, jnp.float32)
    if shards:
        result = result * steps_of(key, extent, shards, -0.22, 0.18)
    return jnp.clip(raised(result, jax.random.fold_in(key, 3), *heavy), -bound, bound).astype(held_as)


def setup_inputs(seed: int = 0) -> dict:
    key_of = jax.random.split(jax.random.key(seed), 9)
    return {
        "grad_out": bell_draw_with(key_of[0], (TOKENS, D), 0.5, 4.0, ((0, 8), (1, 4)), (0, 1, 8, 2.0)),
        "proj_weight": noise(key_of[1], (D, HEADS * HEAD_DIM), (HEADS * HEAD_DIM) ** -0.5, 0.09375, ((0, 8), (1, 4))),
        "queries": draw_queries(jax.random.fold_in(key_of[8], 71), 0),
        "keys": draw_keys(jax.random.fold_in(key_of[8], 71), 0),
        "values": noise(key_of[4], (TOKENS, HEADS * HEAD_DIM), 1.0, 6.0, ((0, 8), (1, 4))),
        "cache_keys": noise(key_of[5], (CACHE, HEADS * HEAD_DIM), 1.0, 6.0, ((0, 8), (1, 4))),
        "cache_values": noise(key_of[6], (CACHE, HEADS * HEAD_DIM), 1.0, 6.0, ((0, 8), (1, 4))),
        "block_table": different_ones(key_of[7], QBLOCKS, CB, KB, 0),
    }


def rounded(array):
    return lax.optimization_barrier(array.astype(jnp.bfloat16))

def reference(grad_out, proj_weight, queries, keys, values, cache_keys, cache_values, block_table):
    width = HEADS * HEAD_DIM
    inverse_root = 1.0 / math.sqrt(HEAD_DIM)
    blocks = TOKENS // BLOCK
    grad_attn = rounded(jnp.dot(grad_out, proj_weight, preferred_element_type=jnp.float32))

    def split(array, count):
        return array.reshape(count, BLOCK, HEADS, HEAD_DIM)
    cache_key_blocks = split(cache_keys, CB)
    cache_value_blocks = split(cache_values, CB)
    positions = jnp.arange(BLOCK, dtype=jnp.int32)
    causal = positions[:, None] >= positions[None, :]
    allowed = jnp.concatenate([jnp.ones((BLOCK, KB * BLOCK), dtype=bool), causal], axis=1)

    def one_block(carry, inputs):
        grad_ck, grad_cv = carry
        query, own_keys, own_values, grad_block, chosen = inputs
        key_list = jnp.concatenate([cache_key_blocks[chosen].reshape(KB * BLOCK, HEADS, HEAD_DIM), own_keys], axis=0)
        value_list = jnp.concatenate([cache_value_blocks[chosen].reshape(KB * BLOCK, HEADS, HEAD_DIM), own_values], axis=0)
        query_f = query.astype(jnp.float32)
        key_f = key_list.astype(jnp.float32)
        value_f = value_list.astype(jnp.float32)
        grad_f = grad_block.astype(jnp.float32)
        scores = jnp.einsum('qhd,khd->hqk', query_f, key_f) * inverse_root
        scores = jnp.where(allowed[None], scores, -jnp.inf)
        row_max = lax.optimization_barrier(jnp.max(scores, axis=-1, keepdims=True))
        weights = jnp.exp(scores - row_max)
        probs = weights / lax.optimization_barrier(jnp.sum(weights, axis=-1, keepdims=True))
        probs_f = rounded(probs).astype(jnp.float32)
        attn_full = jnp.einsum('hqk,khd->qhd', probs_f, value_f)
        delta = lax.optimization_barrier(jnp.sum(grad_f * attn_full, axis=-1))
        grad_probs = jnp.einsum('qhd,khd->hqk', grad_f, value_f)
        grad_scores = probs * (grad_probs - jnp.transpose(delta)[:, :, None])
        scores_f = rounded(grad_scores).astype(jnp.float32)
        grad_query = jnp.einsum('hqk,khd->qhd', scores_f, key_f) * inverse_root
        grad_key_list = jnp.einsum('hqk,qhd->khd', scores_f, query_f) * inverse_root
        grad_value_list = jnp.einsum('hqk,qhd->khd', probs_f, grad_f)
        grad_ck = grad_ck.at[chosen].add(grad_key_list[:KB * BLOCK].reshape(KB, BLOCK, HEADS, HEAD_DIM))
        grad_cv = grad_cv.at[chosen].add(grad_value_list[:KB * BLOCK].reshape(KB, BLOCK, HEADS, HEAD_DIM))
        outputs = (grad_query.astype(jnp.bfloat16), grad_key_list[KB * BLOCK:].astype(jnp.bfloat16), grad_value_list[KB * BLOCK:].astype(jnp.bfloat16), attn_full.astype(jnp.bfloat16))
        return ((grad_ck, grad_cv), outputs)
    start_carry = (jnp.zeros((CB, BLOCK, HEADS, HEAD_DIM), jnp.float32), jnp.zeros((CB, BLOCK, HEADS, HEAD_DIM), jnp.float32))
    inputs = (split(queries, blocks), split(keys, blocks), split(values, blocks), split(grad_attn, blocks), block_table)
    (grad_ck, grad_cv), outputs = lax.scan(one_block, start_carry, inputs)
    grad_q = outputs[0].reshape(TOKENS, width)
    grad_k = outputs[1].reshape(TOKENS, width)
    grad_v = outputs[2].reshape(TOKENS, width)
    attn_out = outputs[3].reshape(TOKENS, width)
    group_rows = TOKENS // N_COL

    def add_group(total, index):
        rows_out = lax.dynamic_slice_in_dim(grad_out, index * group_rows, group_rows, 0)
        rows_attn = lax.dynamic_slice_in_dim(attn_out, index * group_rows, group_rows, 0)
        partial_sum = lax.dot_general(rows_out, rows_attn, (((0,), (0,)), ((), ())), preferred_element_type=jnp.float32)
        return (total + rounded(partial_sum).astype(jnp.float32), None)
    total, unused = lax.scan(add_group, jnp.zeros((D, width), jnp.float32), jnp.arange(N_COL, dtype=jnp.int32))
    grad_weight = total.astype(jnp.bfloat16)
    return (grad_q, grad_k, grad_v, grad_ck.reshape(CACHE, width), grad_cv.reshape(CACHE, width), grad_weight)
```

```python
import math

import jax
import jax.numpy as jnp
from jax import lax
from jax.experimental import pallas as pl
from jax.experimental.pallas import tpu as pltpu
from jax.sharding import PartitionSpec as P

HEAD_DIM = 128
BLOCK = 128
CB = 8
KB = 4
CACHE = 1024


def per_device(grad_out, proj_weight, queries, keys, values, cache_keys, cache_values, block_table):
    tok_rows = grad_out.shape[0]
    local_width = queries.shape[1]
    head_count = local_width // HEAD_DIM
    inverse_root = 1.0 / math.sqrt(HEAD_DIM)
    full_grads = lax.all_gather(grad_out, "row", axis=1, tiled=True)
    columns = full_grads
    grad_sum = jnp.dot(
        columns,
        lax.all_gather(proj_weight, "col", axis=0, tiled=True),
        preferred_element_type=jnp.float32,
    )
    grad_attn = grad_sum.astype(jnp.bfloat16)
    cache_k_all, cache_v_all = (
        lax.all_gather(cache_keys, "col", axis=0, tiled=True),
        lax.all_gather(cache_values, "col", axis=0, tiled=True),
    )
    cache_key_blocks = cache_k_all.reshape(CB, BLOCK, head_count, HEAD_DIM)
    cache_value_blocks = cache_v_all.reshape(CB, BLOCK, head_count, HEAD_DIM)
    blocks_here = tok_rows // BLOCK
    group = math.gcd(blocks_here, max(1, 512 // BLOCK))
    turns = blocks_here // group
    positions = jnp.arange(BLOCK, dtype=jnp.int32)
    causal = positions[:, None] >= positions[None, :]
    allowed = jnp.concatenate([jnp.ones((BLOCK, KB * BLOCK), dtype=bool), causal], axis=1)
    block_ids = jnp.arange(CB, dtype=jnp.int32)

    def to_groups(array):
        return array.reshape(turns, group, BLOCK, head_count, HEAD_DIM)

    def one_group(carry, inputs):
        grad_ck, grad_cv = carry
        query, own_keys, own_values, grad_block, chosen = inputs
        picked_keys = cache_key_blocks[chosen].reshape(group, KB * BLOCK, head_count, HEAD_DIM)
        picked_values = cache_value_blocks[chosen].reshape(group, KB * BLOCK, head_count, HEAD_DIM)
        key_list = jnp.concatenate([picked_keys, own_keys], axis=1)
        value_list = jnp.concatenate([picked_values, own_values], axis=1)
        scores = (
            jnp.einsum("gqhd,gkhd->ghqk", query, key_list, preferred_element_type=jnp.float32)
            * inverse_root
        )
        scores = jnp.where(allowed[None, None], scores, -jnp.inf)
        row_max = jnp.max(scores, axis=-1, keepdims=True)
        weights = jnp.exp(scores - row_max)
        probs = weights / jnp.sum(weights, axis=-1, keepdims=True)
        probs_b = probs.astype(jnp.bfloat16)
        attn_full = jnp.einsum(
            "ghqk,gkhd->gqhd", probs_b, value_list, preferred_element_type=jnp.float32
        )
        grad_probs = jnp.einsum(
            "gqhd,gkhd->ghqk", grad_block, value_list, preferred_element_type=jnp.float32
        )
        delta = jnp.sum(grad_block.astype(jnp.float32) * attn_full, axis=-1)
        delta = jnp.transpose(delta, (0, 2, 1))[..., None]
        grad_scores = (probs * (grad_probs - delta)).astype(jnp.bfloat16)
        grad_query = (
            jnp.einsum("ghqk,gkhd->gqhd", grad_scores, key_list, preferred_element_type=jnp.float32)
            * inverse_root
        )
        grad_key_list = (
            jnp.einsum("ghqk,gqhd->gkhd", grad_scores, query, preferred_element_type=jnp.float32)
            * inverse_root
        )
        grad_value_list = jnp.einsum(
            "ghqk,gqhd->gkhd", probs_b, grad_block, preferred_element_type=jnp.float32
        )
        one_hot = (chosen.reshape(group * KB)[:, None] == block_ids[None, :]).astype(jnp.float32)
        cache_key_part = grad_key_list[:, : KB * BLOCK].reshape(group * KB, BLOCK * local_width)
        cache_value_part = grad_value_list[:, : KB * BLOCK].reshape(group * KB, BLOCK * local_width)
        grad_ck = grad_ck + jnp.dot(one_hot.T, cache_key_part, precision=lax.Precision.HIGHEST)
        grad_cv = grad_cv + jnp.dot(one_hot.T, cache_value_part, precision=lax.Precision.HIGHEST)
        outputs = (
            grad_query.astype(jnp.bfloat16),
            grad_key_list[:, KB * BLOCK :].astype(jnp.bfloat16),
            grad_value_list[:, KB * BLOCK :].astype(jnp.bfloat16),
            attn_full.astype(jnp.bfloat16),
        )
        return ((grad_ck, grad_cv), outputs)

    start_carry = (
        jnp.zeros((CB, BLOCK * local_width), jnp.float32),
        jnp.zeros((CB, BLOCK * local_width), jnp.float32),
    )
    inputs = (
        to_groups(queries),
        to_groups(keys),
        to_groups(values),
        to_groups(grad_attn),
        block_table.reshape(turns, group, KB),
    )
    (grad_ck, grad_cv), outputs = lax.scan(one_group, start_carry, inputs)
    grad_q = outputs[0].reshape(tok_rows, local_width)
    grad_k = outputs[1].reshape(tok_rows, local_width)
    grad_v = outputs[2].reshape(tok_rows, local_width)
    attn_out = outputs[3].reshape(tok_rows, local_width)
    grad_cache_k, grad_cache_v = (
        lax.psum_scatter(
            grad_ck.reshape(CACHE, local_width).astype(jnp.bfloat16),
            "col",
            scatter_dimension=0,
            tiled=True,
        ).astype(jnp.float32),
        lax.psum_scatter(
            grad_cv.reshape(CACHE, local_width).astype(jnp.bfloat16),
            "col",
            scatter_dimension=0,
            tiled=True,
        ).astype(jnp.float32),
    )
    columns = full_grads
    grad_weight = lax.psum_scatter(
        lax.dot_general(
            columns, attn_out, (((0,), (0,)), ((), ())), preferred_element_type=jnp.float32
        ).astype(jnp.bfloat16),
        "col",
        scatter_dimension=0,
        tiled=True,
    )
    return (grad_q, grad_k, grad_v, grad_cache_k, grad_cache_v, grad_weight)


F32 = jnp.float32
BF16 = jnp.bfloat16
INV = 1.0 / math.sqrt(HEAD_DIM)
NZ = 4
NEG = -1e30


def dot_nt(a, b):
    return lax.dot_general(a, b, (((1,), (1,)), ((), ())), preferred_element_type=F32)


def dot_tn(a, b):
    return lax.dot_general(a, b, (((0,), (0,)), ((), ())), preferred_element_type=F32)


def dot_nn(a, b):
    return jnp.dot(a, b, preferred_element_type=F32)


def fused_kernel(
    go, w, cache, q, k, v, bias,
    gq, gk, gv, gc, gw,
    G, wbuf, ckv, abuf, gacc, grecv, ga, rbuf, cpart, crecv, cbuf, pscr, dscr,
    loc_sem, c_up, c_dn, c_rv, c_ps, c_pr, g_s, g_r, w_up, w_dn, w_rv, x_s, x_r,
    r_up, r_dn, r_rv, s_up, s_dn, s_rv,
):
    col = lax.axis_index("col")
    row = lax.axis_index("row")
    z = col // 2
    core = col % 2
    other = 1 - core
    has_up = z < NZ - 1
    has_dn = z > 0
    partner = {"col": z * 2 + other}
    up = {"col": jnp.minimum(col + 2, 2 * NZ - 2 + core)}
    dn = {"col": jnp.maximum(col - 2, core)}
    rx = row + 1 - 2 * (row % 2)
    ry = (row + 2) % 4
    rd = (rx + 2) % 4
    xn = {"row": rx}
    yn = {"row": ry}
    tok = q.shape[0]
    wid = q.shape[1]
    half = wid // 2
    dblk = w.shape[0]
    pending = []

    def rcopy(src, dst, ss, rs, dev):
        return pltpu.make_async_remote_copy(
            src_ref=src, dst_ref=dst, send_sem=ss, recv_sem=rs,
            device_id=dev, device_id_type=pl.DeviceIdType.MESH,
        )

    def when(cond, fn):
        if cond is None:
            fn()
        else:
            pl.when(cond)(fn)

    def send(copy, cond=None):
        when(cond, copy.start)
        pending.append((copy, cond))

    def arrived(ref, sem, cond=None):
        when(cond, lambda: pltpu.make_async_copy(ref, ref, sem).wait())

    barrier = pltpu.get_barrier_semaphore()

    def greet(dev):
        pl.semaphore_signal(barrier, inc=1, device_id=dev, device_id_type=pl.DeviceIdType.MESH)

    for dev in (partner, xn, yn):
        greet(dev)
    pl.when(has_up)(lambda: greet(up))
    pl.when(has_dn)(lambda: greet(dn))
    pl.semaphore_wait(barrier, 3 + jnp.where(has_up, 1, 0) + jnp.where(has_dn, 1, 0))

    send(rcopy(cache, ckv.at[z, core], c_up.at[0], c_rv.at[z], up), has_up)
    send(rcopy(cache, ckv.at[z, core], c_dn.at[0], c_rv.at[z], dn), has_dn)
    send(rcopy(cache, ckv.at[z, core], c_ps.at[0], c_pr.at[z], partner))
    mine = pl.ds(pl.multiple_of(core * dblk, dblk), dblk)
    theirs = pl.ds(pl.multiple_of(other * dblk, dblk), dblk)
    trow = pl.ds(pl.multiple_of(core * tok, tok), tok)
    orow = pl.ds(pl.multiple_of(other * tok, tok), tok)
    send(rcopy(go.at[:, theirs], G.at[row, trow], g_s.at[0], g_r.at[0], partner))
    send(rcopy(go.at[:, mine], G.at[row, trow], g_s.at[1], g_r.at[1 + core], xn))
    send(rcopy(go.at[:, mine], G.at[row, trow], g_s.at[2], g_r.at[3 + core], yn))

    locals_ = [
        pltpu.make_async_copy(cache, ckv.at[z, core], loc_sem.at[0]),
        pltpu.make_async_copy(go.at[:, mine], G.at[row, trow], loc_sem.at[1]),
        pltpu.make_async_copy(w.at[:, pl.ds(0, half)], wbuf.at[z, 0], loc_sem.at[2]),
        pltpu.make_async_copy(w.at[:, pl.ds(half, half)], wbuf.at[z, 1], loc_sem.at[3]),
    ]
    for c in locals_:
        c.start()

    def cache_step(t):
        below, above = z - t, z + t
        lo, hi = jnp.maximum(below, 0), jnp.minimum(above, NZ - 1)
        got_lo, got_hi = below >= 0, above < NZ
        arrived(ckv.at[lo, core], c_rv.at[lo], got_lo)
        if t < NZ - 1:
            send(rcopy(ckv.at[lo, core], ckv.at[lo, core], c_up.at[t], c_rv.at[lo], up),
                 jnp.logical_and(got_lo, has_up))
        send(rcopy(ckv.at[lo, core], ckv.at[lo, core], c_ps.at[2 * t - 1], c_pr.at[lo], partner), got_lo)
        arrived(ckv.at[hi, core], c_rv.at[hi], got_hi)
        if t < NZ - 1:
            send(rcopy(ckv.at[hi, core], ckv.at[hi, core], c_dn.at[t], c_rv.at[hi], dn),
                 jnp.logical_and(got_hi, has_dn))
        send(rcopy(ckv.at[hi, core], ckv.at[hi, core], c_ps.at[2 * t], c_pr.at[hi], partner), got_hi)

    def w_own(h):
        src = w.at[:, pl.ds(h * half, half)]
        send(rcopy(src, wbuf.at[z, h], w_up.at[0, h], w_rv.at[z, h], up), has_up)
        send(rcopy(src, wbuf.at[z, h], w_dn.at[0, h], w_rv.at[z, h], dn), has_dn)

    def w_step(t, h):
        below, above = z - t, z + t
        lo, hi = jnp.maximum(below, 0), jnp.minimum(above, NZ - 1)
        got_lo, got_hi = below >= 0, above < NZ
        arrived(wbuf.at[lo, h], w_rv.at[lo, h], got_lo)
        if t < NZ - 1:
            send(rcopy(wbuf.at[lo, h], wbuf.at[lo, h], w_up.at[t, h], w_rv.at[lo, h], up),
                 jnp.logical_and(got_lo, has_up))
        arrived(wbuf.at[hi, h], w_rv.at[hi, h], got_hi)
        if t < NZ - 1:
            send(rcopy(wbuf.at[hi, h], wbuf.at[hi, h], w_dn.at[t, h], w_rv.at[hi, h], dn),
                 jnp.logical_and(got_hi, has_dn))

    def clear(s):
        rbuf[s] = jnp.zeros(rbuf.shape[1:], BF16)
        for h in range(2):
            cbuf[h, s] = jnp.zeros(cbuf.shape[2:], BF16)

    @pl.when(z == 0)
    def _():
        lax.fori_loop(0, NZ, lambda s, c: (clear(s), c)[1], 0)

    @pl.when(z == NZ - 1)
    def _():
        lax.fori_loop(0, NZ - 1, lambda s, c: (clear(s), c)[1], 0)
        clear(NZ)

    cache_step(1)
    w_own(0)
    arrived(G.at[row, orow], g_r.at[0])
    send(rcopy(G.at[row, orow], G.at[row, orow], g_s.at[3], g_r.at[1 + other], xn))
    send(rcopy(G.at[row, orow], G.at[row, orow], g_s.at[4], g_r.at[3 + other], yn))
    cache_step(2)
    cache_step(3)
    for c in locals_:
        c.wait()
    for s in range(NZ):
        arrived(ckv.at[s, other], c_pr.at[s])

    causal = (lax.broadcasted_iota(jnp.int32, (BLOCK, BLOCK), 0)
              >= lax.broadcasted_iota(jnp.int32, (BLOCK, BLOCK), 1))
    blocks = tok // BLOCK

    def head_cols(h):
        return pl.ds(pl.multiple_of(h * HEAD_DIM, HEAD_DIM), HEAD_DIM)

    def cached(kv, cols):
        return ckv[:, :, kv, :, cols].reshape(CACHE, HEAD_DIM)

    def probs_of(b, cols, kc):
        rows = pl.ds(b * BLOCK, BLOCK)
        qb = q[rows, cols]
        s1 = dot_nt(qb, kc) * INV + bias[b]
        s2 = jnp.where(causal, dot_nt(qb, k[rows, cols]) * INV, NEG)
        m = jnp.maximum(jnp.max(s1, axis=1, keepdims=True), jnp.max(s2, axis=1, keepdims=True))
        e1 = jnp.exp(s1 - m)
        e2 = jnp.exp(s2 - m)
        r = 1.0 / (jnp.sum(e1, axis=1, keepdims=True) + jnp.sum(e2, axis=1, keepdims=True))
        return e1 * r, e2 * r

    def fwd_head(h, c):
        cols = head_cols(h)
        kc = cached(0, cols)
        vc = cached(1, cols)
        for b in range(blocks):
            rows = pl.ds(b * BLOCK, BLOCK)
            p1, p2 = probs_of(b, cols, kc)
            o = dot_nn(p1.astype(BF16), vc) + dot_nn(p2.astype(BF16), v[rows, cols])
            abuf[pl.ds(pl.multiple_of(core * tok + b * BLOCK, BLOCK), BLOCK), cols] = o.astype(BF16)
        return c

    lax.fori_loop(0, wid // HEAD_DIM, fwd_head, 0)
    send(rcopy(abuf.at[trow], abuf.at[trow], x_s.at[0], x_r.at[0], partner))

    w_step(1, 0)
    w_own(1)

    first, second = pl.ds(0, tok), pl.ds(tok, tok)
    arrived(G.at[rx, first], g_r.at[1])
    send(rcopy(G.at[rx, first], G.at[rx, first], g_s.at[5], g_r.at[5], yn))
    arrived(G.at[ry, second], g_r.at[4])
    send(rcopy(G.at[ry, second], G.at[ry, second], g_s.at[6], g_r.at[6], xn))
    arrived(G.at[rx, second], g_r.at[2])
    arrived(G.at[ry, first], g_r.at[3])
    w_step(2, 0)
    arrived(G.at[rd, first], g_r.at[5])
    arrived(G.at[rd, second], g_r.at[6])
    arrived(abuf.at[orow], x_r.at[0])

    tile = 256

    def wg_tile(zd, h, n):
        rows = pl.ds(pl.multiple_of(n * tile, tile), tile)
        return rows, dot_tn(G[zd, :, rows], abuf[:, pl.ds(h * half, half)])

    def rs_step(t, h):
        zu = NZ - 1 - t + z
        go_up = jnp.logical_and(zu > z, zu < NZ)
        su = jnp.clip(zu, 0, NZ - 1)
        zl = t - (NZ - 1) + z
        go_dn = jnp.logical_and(zl >= 0, zl < z)
        sl = jnp.clip(zl, 0, NZ - 1)
        for go_, s, got, sems, dev, dst in (
            (go_up, su, has_dn, r_up, up, su),
            (go_dn, sl, has_up, r_dn, dn, jnp.where(zl == z - 1, NZ, sl)),
        ):
            arrived(rbuf.at[s, h], r_rv.at[s, h], jnp.logical_and(go_, got))

            @pl.when(go_)
            def _(s=s):
                def body(n, c):
                    rows, part = wg_tile(s, h, n)
                    rbuf[s, h, rows, :] = (rbuf[s, h, rows, :].astype(F32) + part).astype(BF16)
                    return c
                lax.fori_loop(0, dblk // tile, body, 0)

            send(rcopy(rbuf.at[s, h], rbuf.at[dst, h], sems.at[t, h], r_rv.at[dst, h], dev), go_)

    def ga_part(h):
        def body(n, c):
            rows = pl.ds(pl.multiple_of(n * tile, tile), tile)
            acc = dot_nn(G[0, rows, :], wbuf[0, h])
            for s in range(1, NZ):
                acc = acc + dot_nn(G[s, rows, :], wbuf[s, h])
            gacc[h, rows, :] = acc
            return c
        lax.fori_loop(0, 2 * tok // tile, body, 0)
        send(rcopy(gacc.at[h, orow], grecv.at[h], x_s.at[1 + h], x_r.at[1 + h], partner))

    def bwd(h):
        arrived(grecv.at[h], x_r.at[1 + h])
        ga[...] = (gacc[h, trow, :] + grecv[h]).astype(BF16)

        def head(j, c):
            cols = head_cols(h * (half // HEAD_DIM) + j)
            jc = head_cols(j)
            kc = cached(0, cols)
            vc = cached(1, cols)
            for b in range(blocks):
                rows = pl.ds(b * BLOCK, BLOCK)
                p1, p2 = probs_of(b, cols, kc)
                gb = ga[rows, jc]
                d1 = dot_nt(gb, vc)
                d2 = dot_nt(gb, v[rows, cols])
                b1 = p1.astype(BF16)
                b2 = p2.astype(BF16)
                delta = (jnp.sum(b1.astype(F32) * d1, axis=1, keepdims=True)
                         + jnp.sum(b2.astype(F32) * d2, axis=1, keepdims=True))
                t1 = (p1 * (d1 - delta)).astype(BF16)
                t2 = (p2 * (d2 - delta)).astype(BF16)
                pscr[rows, :] = b1
                dscr[rows, :] = t1
                kb = k[rows, cols]
                gq[rows, cols] = ((dot_nn(t1, kc) + dot_nn(t2, kb)) * INV).astype(BF16)
                gk[rows, cols] = (dot_tn(t2, q[rows, cols]) * INV).astype(BF16)
                gv[rows, cols] = dot_tn(b2, gb).astype(BF16)
            ck = (dot_tn(dscr[...], q[:, cols]) * INV).astype(BF16)
            cv = dot_tn(pscr[...], ga[:, jc]).astype(BF16)
            for kv, part in ((0, ck), (1, cv)):
                part = part.reshape(NZ, 2, BLOCK, HEAD_DIM)
                for s in range(NZ):
                    for side in range(2):
                        cpart[h, side, s, kv, :, jc] = part[s, side]
            return c

        lax.fori_loop(0, half // HEAD_DIM, head, 0)
        send(rcopy(cpart.at[h, other], crecv.at[h], x_s.at[3 + h], x_r.at[3 + h], partner))

    def pair_sum(h):
        arrived(crecv.at[h], x_r.at[3 + h])

    def cache_sum(h, s):
        return cpart[h, core, s].astype(F32) + crecv[h, s].astype(F32)

    def crs_step(t, h):
        zu = NZ - 1 - t + z
        go_up = jnp.logical_and(zu > z, zu < NZ)
        su = jnp.clip(zu, 0, NZ - 1)
        zl = t - (NZ - 1) + z
        go_dn = jnp.logical_and(zl >= 0, zl < z)
        sl = jnp.clip(zl, 0, NZ - 1)
        for go_, s, got, sems, dev, dst in (
            (go_up, su, has_dn, s_up, up, su),
            (go_dn, sl, has_up, s_dn, dn, jnp.where(zl == z - 1, NZ, sl)),
        ):
            arrived(cbuf.at[h, s], s_rv.at[s, h], jnp.logical_and(go_, got))

            @pl.when(go_)
            def _(s=s):
                cbuf[h, s] = (cbuf[h, s].astype(F32) + cache_sum(h, s)).astype(BF16)

            send(rcopy(cbuf.at[h, s], cbuf.at[h, dst], sems.at[t, h], s_rv.at[dst, h], dev), go_)

    rs_step(0, 0)
    rs_step(0, 1)
    w_step(3, 0)
    ga_part(0)
    w_step(1, 1)
    rs_step(1, 0)
    bwd(0)
    w_step(2, 1)
    rs_step(1, 1)
    pair_sum(0)
    crs_step(0, 0)
    rs_step(2, 0)
    crs_step(1, 0)
    rs_step(2, 1)
    w_step(3, 1)
    ga_part(1)
    crs_step(2, 0)
    bwd(1)
    pair_sum(1)
    for t in range(NZ - 1):
        crs_step(t, 1)

    for h in range(2):
        arrived(rbuf.at[z, h], r_rv.at[z, h], has_dn)
        arrived(rbuf.at[NZ, h], r_rv.at[NZ, h], has_up)

        def last(n, c, h=h):
            rows, part = wg_tile(z, h, n)
            total = part + rbuf[z, h, rows, :].astype(F32) + rbuf[NZ, h, rows, :].astype(F32)
            gw[rows, pl.ds(h * half, half)] = total.astype(BF16)
            return c

        lax.fori_loop(0, dblk // tile, last, 0)
    for h in range(2):
        arrived(cbuf.at[h, z], s_rv.at[z, h], has_dn)
        arrived(cbuf.at[h, NZ], s_rv.at[NZ, h], has_up)
        gc[:, :, pl.ds(h * half, half)] = (
            cache_sum(h, z) + cbuf[h, z].astype(F32) + cbuf[h, NZ].astype(F32)
        )

    for copy, cond in pending:
        when(cond, copy.wait_send)


def per_device_fused(grad_out, proj_weight, queries, keys, values, cache_keys, cache_values, block_table):
    tok, wid = queries.shape
    half = wid // 2
    dblk = proj_weight.shape[0]
    blocks = tok // BLOCK
    cache = jnp.stack([cache_keys, cache_values])
    named = jnp.any(block_table[:, :, None] == jnp.arange(CB, dtype=jnp.int32), axis=1)
    bias = jnp.repeat(jnp.where(named, 0.0, NEG).astype(F32), BLOCK, axis=1).reshape(blocks, 1, CACHE)
    vm = pl.BlockSpec(memory_space=pltpu.VMEM)
    hbm = pl.BlockSpec(memory_space=pl.ANY)
    dma = pltpu.SemaphoreType.DMA
    out = pl.pallas_call(
        fused_kernel,
        out_shape=(
            jax.ShapeDtypeStruct((tok, wid), BF16),
            jax.ShapeDtypeStruct((tok, wid), BF16),
            jax.ShapeDtypeStruct((tok, wid), BF16),
            jax.ShapeDtypeStruct((2, BLOCK, wid), F32),
            jax.ShapeDtypeStruct((dblk, wid), BF16),
        ),
        in_specs=[hbm, hbm, hbm, vm, vm, vm, vm],
        out_specs=[vm] * 5,
        scratch_shapes=[
            pltpu.VMEM((NZ, 2 * tok, dblk), BF16),
            pltpu.VMEM((NZ, 2, dblk, half), BF16),
            pltpu.VMEM((NZ, 2, 2, BLOCK, wid), BF16),
            pltpu.VMEM((2 * tok, wid), BF16),
            pltpu.VMEM((2, 2 * tok, half), F32),
            pltpu.VMEM((2, tok, half), F32),
            pltpu.VMEM((tok, half), BF16),
            pltpu.VMEM((NZ + 1, 2, dblk, half), BF16),
            pltpu.VMEM((2, 2, NZ, 2, BLOCK, half), BF16),
            pltpu.VMEM((2, NZ, 2, BLOCK, half), BF16),
            pltpu.VMEM((2, NZ + 1, 2, BLOCK, half), BF16),
            pltpu.VMEM((tok, CACHE), BF16),
            pltpu.VMEM((tok, CACHE), BF16),
            dma((4,)), dma((3,)), dma((3,)), dma((NZ,)), dma((7,)), dma((NZ,)),
            dma((7,)), dma((7,)),
            dma((3, 2)), dma((3, 2)), dma((NZ, 2)),
            dma((5,)), dma((5,)),
            dma((3, 2)), dma((3, 2)), dma((NZ + 1, 2)),
            dma((3, 2)), dma((3, 2)), dma((NZ + 1, 2)),
        ],
        compiler_params=pltpu.CompilerParams(
            collective_id=0, has_side_effects=True, vmem_limit_bytes=64 * 1024 * 1024
        ),
        name="fused",
    )(grad_out, proj_weight, cache, queries, keys, values, bias)
    return out[0], out[1], out[2], out[3][0], out[3][1], out[4]


def fits_fused(mesh):
    return mesh.shape["row"] == 4 and mesh.shape["col"] == 2 * NZ


def solution(mesh):
    in_specs = (
        P("col", "row"),
        P("col", "row"),
        P("col", "row"),
        P("col", "row"),
        P("col", "row"),
        P("col", "row"),
        P("col", "row"),
        P("col", None),
    )
    out_specs = (
        P("col", "row"),
        P("col", "row"),
        P("col", "row"),
        P("col", "row"),
        P("col", "row"),
        P("col", "row"),
    )
    return jax.shard_map(
        per_device_fused if fits_fused(mesh) else per_device, mesh=mesh, in_specs=in_specs, out_specs=out_specs, check_vma=False
    )
```

```python
import math

import jax
import jax.numpy as jnp
from jax import lax
from jax.experimental import pallas as pl
from jax.experimental.pallas import tpu as pltpu
from jax.sharding import PartitionSpec as P

HEAD_DIM = 128
BLOCK = 128
CB = 8
KB = 4
CACHE = 1024


def per_device(grad_out, proj_weight, queries, keys, values, cache_keys, cache_values, block_table):
    tok_rows = grad_out.shape[0]
    local_width = queries.shape[1]
    head_count = local_width // HEAD_DIM
    inverse_root = 1.0 / math.sqrt(HEAD_DIM)
    full_grads = lax.all_gather(grad_out, "row", axis=1, tiled=True)
    columns = full_grads
    grad_sum = jnp.dot(
        columns,
        lax.all_gather(proj_weight, "col", axis=0, tiled=True),
        preferred_element_type=jnp.float32,
    )
    grad_attn = grad_sum.astype(jnp.bfloat16)
    cache_k_all, cache_v_all = (
        lax.all_gather(cache_keys, "col", axis=0, tiled=True),
        lax.all_gather(cache_values, "col", axis=0, tiled=True),
    )
    cache_key_blocks = cache_k_all.reshape(CB, BLOCK, head_count, HEAD_DIM)
    cache_value_blocks = cache_v_all.reshape(CB, BLOCK, head_count, HEAD_DIM)
    blocks_here = tok_rows // BLOCK
    group = math.gcd(blocks_here, max(1, 512 // BLOCK))
    turns = blocks_here // group
    positions = jnp.arange(BLOCK, dtype=jnp.int32)
    causal = positions[:, None] >= positions[None, :]
    allowed = jnp.concatenate([jnp.ones((BLOCK, KB * BLOCK), dtype=bool), causal], axis=1)
    block_ids = jnp.arange(CB, dtype=jnp.int32)

    def to_groups(array):
        return array.reshape(turns, group, BLOCK, head_count, HEAD_DIM)

    def one_group(carry, inputs):
        grad_ck, grad_cv = carry
        query, own_keys, own_values, grad_block, chosen = inputs
        picked_keys = cache_key_blocks[chosen].reshape(group, KB * BLOCK, head_count, HEAD_DIM)
        picked_values = cache_value_blocks[chosen].reshape(group, KB * BLOCK, head_count, HEAD_DIM)
        key_list = jnp.concatenate([picked_keys, own_keys], axis=1)
        value_list = jnp.concatenate([picked_values, own_values], axis=1)
        scores = (
            jnp.einsum("gqhd,gkhd->ghqk", query, key_list, preferred_element_type=jnp.float32)
            * inverse_root
        )
        scores = jnp.where(allowed[None, None], scores, -jnp.inf)
        row_max = jnp.max(scores, axis=-1, keepdims=True)
        weights = jnp.exp(scores - row_max)
        probs = weights / jnp.sum(weights, axis=-1, keepdims=True)
        probs_b = probs.astype(jnp.bfloat16)
        attn_full = jnp.einsum(
            "ghqk,gkhd->gqhd", probs_b, value_list, preferred_element_type=jnp.float32
        )
        grad_probs = jnp.einsum(
            "gqhd,gkhd->ghqk", grad_block, value_list, preferred_element_type=jnp.float32
        )
        delta = jnp.sum(grad_block.astype(jnp.float32) * attn_full, axis=-1)
        delta = jnp.transpose(delta, (0, 2, 1))[..., None]
        grad_scores = (probs * (grad_probs - delta)).astype(jnp.bfloat16)
        grad_query = (
            jnp.einsum("ghqk,gkhd->gqhd", grad_scores, key_list, preferred_element_type=jnp.float32)
            * inverse_root
        )
        grad_key_list = (
            jnp.einsum("ghqk,gqhd->gkhd", grad_scores, query, preferred_element_type=jnp.float32)
            * inverse_root
        )
        grad_value_list = jnp.einsum(
            "ghqk,gqhd->gkhd", probs_b, grad_block, preferred_element_type=jnp.float32
        )
        one_hot = (chosen.reshape(group * KB)[:, None] == block_ids[None, :]).astype(jnp.float32)
        cache_key_part = grad_key_list[:, : KB * BLOCK].reshape(group * KB, BLOCK * local_width)
        cache_value_part = grad_value_list[:, : KB * BLOCK].reshape(group * KB, BLOCK * local_width)
        grad_ck = grad_ck + jnp.dot(one_hot.T, cache_key_part, precision=lax.Precision.HIGHEST)
        grad_cv = grad_cv + jnp.dot(one_hot.T, cache_value_part, precision=lax.Precision.HIGHEST)
        outputs = (
            grad_query.astype(jnp.bfloat16),
            grad_key_list[:, KB * BLOCK :].astype(jnp.bfloat16),
            grad_value_list[:, KB * BLOCK :].astype(jnp.bfloat16),
            attn_full.astype(jnp.bfloat16),
        )
        return ((grad_ck, grad_cv), outputs)

    start_carry = (
        jnp.zeros((CB, BLOCK * local_width), jnp.float32),
        jnp.zeros((CB, BLOCK * local_width), jnp.float32),
    )
    inputs = (
        to_groups(queries),
        to_groups(keys),
        to_groups(values),
        to_groups(grad_attn),
        block_table.reshape(turns, group, KB),
    )
    (grad_ck, grad_cv), outputs = lax.scan(one_group, start_carry, inputs)
    grad_q = outputs[0].reshape(tok_rows, local_width)
    grad_k = outputs[1].reshape(tok_rows, local_width)
    grad_v = outputs[2].reshape(tok_rows, local_width)
    attn_out = outputs[3].reshape(tok_rows, local_width)
    grad_cache_k, grad_cache_v = (
        lax.psum_scatter(
            grad_ck.reshape(CACHE, local_width).astype(jnp.bfloat16),
            "col",
            scatter_dimension=0,
            tiled=True,
        ).astype(jnp.float32),
        lax.psum_scatter(
            grad_cv.reshape(CACHE, local_width).astype(jnp.bfloat16),
            "col",
            scatter_dimension=0,
            tiled=True,
        ).astype(jnp.float32),
    )
    columns = full_grads
    grad_weight = lax.psum_scatter(
        lax.dot_general(
            columns, attn_out, (((0,), (0,)), ((), ())), preferred_element_type=jnp.float32
        ).astype(jnp.bfloat16),
        "col",
        scatter_dimension=0,
        tiled=True,
    )
    return (grad_q, grad_k, grad_v, grad_cache_k, grad_cache_v, grad_weight)


F32 = jnp.float32
BF16 = jnp.bfloat16
INV = 1.0 / math.sqrt(HEAD_DIM)
NZ = 4
NEG = -1e30


def dot_nt(a, b):
    return lax.dot_general(a, b, (((1,), (1,)), ((), ())), preferred_element_type=F32)


def dot_tn(a, b):
    return lax.dot_general(a, b, (((0,), (0,)), ((), ())), preferred_element_type=F32)


def dot_nn(a, b):
    return jnp.dot(a, b, preferred_element_type=F32)


def fused_kernel(
    go, w, cache, q, k, v, bias,
    gq, gk, gv, gc, gw, H, gx,
    G, ckv, abuf, gpart, grecv, ga, rbuf, cpart, crecv, cbuf, pscr, dscr,
    loc_sem, c_up, c_dn, c_rv, c_ps, c_pr, a_up, a_dn, a_rv, a_ps, a_pr,
    g_s, g_r, p_s, p_r, x_s, x_r, r_up, r_dn, r_rv, s_up, s_dn, s_rv,
):
    col = lax.axis_index("col")
    row = lax.axis_index("row")
    z = col // 2
    core = col % 2
    other = 1 - core
    has_up = z < NZ - 1
    has_dn = z > 0
    partner = {"col": z * 2 + other}
    up = {"col": jnp.minimum(col + 2, 2 * NZ - 2 + core)}
    dn = {"col": jnp.maximum(col - 2, core)}
    rx = row + 1 - 2 * (row % 2)
    ry = (row + 2) % 4
    rd = (rx + 2) % 4
    xn = {"row": rx}
    yn = {"row": ry}
    dg = {"row": rd}
    tok = q.shape[0]
    wid = q.shape[1]
    half = wid // 2
    dblk = w.shape[0]
    pending = []

    def rcopy(src, dst, ss, rs, dev):
        return pltpu.make_async_remote_copy(
            src_ref=src, dst_ref=dst, send_sem=ss, recv_sem=rs,
            device_id=dev, device_id_type=pl.DeviceIdType.MESH,
        )

    def when(cond, fn):
        if cond is None:
            fn()
        else:
            pl.when(cond)(fn)

    def send(copy, cond=None):
        when(cond, copy.start)
        pending.append((copy, cond))

    def arrived(ref, sem, cond=None):
        when(cond, lambda: pltpu.make_async_copy(ref, ref, sem).wait())

    barrier = pltpu.get_barrier_semaphore()

    def greet(dev):
        pl.semaphore_signal(barrier, inc=1, device_id=dev, device_id_type=pl.DeviceIdType.MESH)

    zs_of = [(z + NZ - i) % NZ for i in range(NZ)]
    zd_of = [(z + i) % NZ for i in range(NZ)]
    line = [{"col": zd_of[i] * 2 + core} for i in range(NZ)]
    for dev in (partner, xn, yn, dg, line[1], line[2], line[3]):
        greet(dev)
    pl.semaphore_wait(barrier, 7)

    def line_own(src, buf, sems):
        s_u, s_d, rv, ps, pr = sems
        send(rcopy(src, buf.at[z, core], s_u.at[0], rv.at[z], up), has_up)
        send(rcopy(src, buf.at[z, core], s_d.at[0], rv.at[z], dn), has_dn)
        send(rcopy(src, buf.at[z, core], ps.at[0], pr.at[z], partner))

    def line_step(t, buf, sems):
        s_u, s_d, rv, ps, pr = sems
        below, above = z - t, z + t
        lo, hi = jnp.maximum(below, 0), jnp.minimum(above, NZ - 1)
        got_lo, got_hi = below >= 0, above < NZ
        for s, got, hop, ss, dev, n in (
            (lo, got_lo, has_up, s_u, up, 2 * t - 1),
            (hi, got_hi, has_dn, s_d, dn, 2 * t),
        ):
            piece = buf.at[s, core]
            arrived(piece, rv.at[s], got)
            if t < NZ - 1:
                send(rcopy(piece, piece, ss.at[t], rv.at[s], dev), jnp.logical_and(got, hop))
            send(rcopy(piece, piece, ps.at[n], pr.at[s], partner), got)

    c_sems = (c_up, c_dn, c_rv, c_ps, c_pr)
    a_sems = (a_up, a_dn, a_rv, a_ps, a_pr)
    line_own(cache, ckv, c_sems)
    mine = pl.ds(pl.multiple_of(core * dblk, dblk), dblk)
    theirs = pl.ds(pl.multiple_of(other * dblk, dblk), dblk)
    send(rcopy(go.at[:, theirs], gx, g_s.at[0], g_r.at[0], partner))

    def quarter(r):
        return pl.ds(pl.multiple_of(r * BLOCK, BLOCK), BLOCK)

    plane = ((rx, xn), (ry, yn), (rd, dg))
    for n, (r, dev) in enumerate(plane):
        send(rcopy(go.at[quarter(r), mine], H.at[row, core], g_s.at[1 + n], g_r.at[1 + 2 * n + core], dev))

    locals_ = [
        pltpu.make_async_copy(cache, ckv.at[z, core], loc_sem.at[0]),
        pltpu.make_async_copy(go.at[quarter(row), mine], H.at[row, core], loc_sem.at[1]),
    ]
    for c in locals_:
        c.start()

    def clear(s):
        rbuf[s] = jnp.zeros(rbuf.shape[1:], BF16)
        for h in range(2):
            cbuf[h, s] = jnp.zeros(cbuf.shape[2:], BF16)

    @pl.when(z == 0)
    def _():
        lax.fori_loop(0, NZ, lambda s, c: (clear(s), c)[1], 0)

    @pl.when(z == NZ - 1)
    def _():
        lax.fori_loop(0, NZ - 1, lambda s, c: (clear(s), c)[1], 0)
        clear(NZ)

    line_step(1, ckv, c_sems)
    arrived(gx, g_r.at[0])
    for n, (r, dev) in enumerate(plane):
        send(rcopy(gx.at[quarter(r)], H.at[row, other], g_s.at[4 + n], g_r.at[1 + 2 * n + other], dev))
    own_gx = pltpu.make_async_copy(gx.at[quarter(row)], H.at[row, other], loc_sem.at[2])
    own_gx.start()
    line_step(2, ckv, c_sems)
    for c in locals_:
        c.wait()
    own_gx.wait()
    for n, (r, dev) in enumerate(plane):
        for side in range(2):
            arrived(H.at[r, side], g_r.at[1 + 2 * n + side])
    own_h = pltpu.make_async_copy(H.at[z], G.at[z, :, row], loc_sem.at[3])
    own_h.start()
    for i in range(1, NZ):
        send(rcopy(H.at[zd_of[i]], G.at[z, :, row], g_s.at[6 + i], g_r.at[6 + i], line[i]))

    def plane_send(i):
        piece = G.at[zs_of[i], :, row]
        if i == 0:
            own_h.wait()
        else:
            arrived(piece, g_r.at[6 + i])
        send(rcopy(piece, piece, g_s.at[10 + i], g_r.at[10 + i], xn))
        send(rcopy(piece, piece, g_s.at[14 + i], g_r.at[14 + i], yn))

    def plane_pass(i):
        zs = zs_of[i]
        arrived(G.at[zs, :, rx], g_r.at[10 + i])
        send(rcopy(G.at[zs, 0, rx], G.at[zs, 0, rx], g_s.at[18 + i], g_r.at[18 + i], yn))
        arrived(G.at[zs, :, ry], g_r.at[14 + i])
        send(rcopy(G.at[zs, 1, ry], G.at[zs, 1, ry], g_s.at[22 + i], g_r.at[22 + i], xn))

    plane_send(0)
    line_step(3, ckv, c_sems)
    for s in range(NZ):
        arrived(ckv.at[s, other], c_pr.at[s])

    causal = (lax.broadcasted_iota(jnp.int32, (BLOCK, BLOCK), 0)
              >= lax.broadcasted_iota(jnp.int32, (BLOCK, BLOCK), 1))
    blocks = tok // BLOCK

    def head_cols(h):
        return pl.ds(pl.multiple_of(h * HEAD_DIM, HEAD_DIM), HEAD_DIM)

    def cached(kv, cols):
        return ckv[:, :, kv, :, cols].reshape(CACHE, HEAD_DIM)

    def probs_of(b, cols, kc):
        rows = pl.ds(b * BLOCK, BLOCK)
        qb = q[rows, cols]
        s1 = dot_nt(qb, kc) * INV + bias[b]
        s2 = jnp.where(causal, dot_nt(qb, k[rows, cols]) * INV, NEG)
        m = jnp.maximum(jnp.max(s1, axis=1, keepdims=True), jnp.max(s2, axis=1, keepdims=True))
        e1 = jnp.exp(s1 - m)
        e2 = jnp.exp(s2 - m)
        r = 1.0 / (jnp.sum(e1, axis=1, keepdims=True) + jnp.sum(e2, axis=1, keepdims=True))
        return e1 * r, e2 * r

    def fwd_head(h, c):
        cols = head_cols(h)
        kc = cached(0, cols)
        vc = cached(1, cols)
        for b in range(blocks):
            rows = pl.ds(b * BLOCK, BLOCK)
            p1, p2 = probs_of(b, cols, kc)
            o = dot_nn(p1.astype(BF16), vc) + dot_nn(p2.astype(BF16), v[rows, cols])
            abuf[z, core, rows, cols] = o.astype(BF16)
        return c

    lax.fori_loop(0, wid // HEAD_DIM, fwd_head, 0)
    line_own(abuf.at[z, core], abuf, a_sems)

    tile = 256

    def ga_part(i):
        zs = zs_of[i]
        arrived(G.at[zs, 0, rd], g_r.at[18 + i])
        arrived(G.at[zs, 1, rd], g_r.at[22 + i])

        def body(n, c):
            side = n // 2
            part = n % 2
            rows = pl.ds(pl.multiple_of(part * tile, tile), tile)
            lhs = G[zs, side, pl.ds(part * 2, 2)].reshape(tile, dblk)
            for h in range(2):
                acc = dot_nn(lhs, w[:, pl.ds(h * half, half)])
                gpart[side, zs, h, rows, :] = acc.astype(BF16)
            return c

        lax.fori_loop(0, 4, body, 0)
        send(rcopy(gpart.at[other, zs], grecv.at[zs], p_s.at[i], p_r.at[i], partner))

    def gw_tile(n):
        rows = pl.ds(n * tile, tile)
        acc = None
        for s in range(NZ):
            lhs = G[s, :, :, :, rows].reshape(2 * tok, tile)
            part = dot_tn(lhs, abuf[s].reshape(2 * tok, wid))
            acc = part if acc is None else acc + part
        gw[rows, :] = acc.astype(BF16)

    def ga_sum(s, h, rows):
        return (gpart[core, s, h, rows, :].astype(F32) + grecv[s, h, rows, :].astype(F32)
                + rbuf[s, h, rows, :].astype(F32))

    def rs_step(t, h):
        zu = NZ - 1 - t + z
        go_up = jnp.logical_and(zu > z, zu < NZ)
        su = jnp.clip(zu, 0, NZ - 1)
        zl = t - (NZ - 1) + z
        go_dn = jnp.logical_and(zl >= 0, zl < z)
        sl = jnp.clip(zl, 0, NZ - 1)
        for go_, s, got, sems, dev, dst in (
            (go_up, su, has_dn, r_up, up, su),
            (go_dn, sl, has_up, r_dn, dn, jnp.where(zl == z - 1, NZ, sl)),
        ):
            arrived(rbuf.at[s, h], r_rv.at[s, h], jnp.logical_and(go_, got))

            @pl.when(go_)
            def _(s=s):
                def body(n, c):
                    rows = pl.ds(pl.multiple_of(n * BLOCK, BLOCK), BLOCK)
                    rbuf[s, h, rows, :] = ga_sum(s, h, rows).astype(BF16)
                    return c
                lax.fori_loop(0, tok // BLOCK, body, 0)

            send(rcopy(rbuf.at[s, h], rbuf.at[dst, h], sems.at[t, h], r_rv.at[dst, h], dev), go_)

    def bwd(h):
        arrived(rbuf.at[z, h], r_rv.at[z, h], has_dn)
        arrived(rbuf.at[NZ, h], r_rv.at[NZ, h], has_up)

        def total(n, c):
            rows = pl.ds(pl.multiple_of(n * BLOCK, BLOCK), BLOCK)
            ga[rows, :] = (ga_sum(z, h, rows) + rbuf[NZ, h, rows, :].astype(F32)).astype(BF16)
            return c

        lax.fori_loop(0, blocks, total, 0)

        def head(j, c):
            cols = head_cols(h * (half // HEAD_DIM) + j)
            jc = head_cols(j)
            kc = cached(0, cols)
            vc = cached(1, cols)
            for b in range(blocks):
                rows = pl.ds(b * BLOCK, BLOCK)
                p1, p2 = probs_of(b, cols, kc)
                gb = ga[rows, jc]
                d1 = dot_nt(gb, vc)
                d2 = dot_nt(gb, v[rows, cols])
                b1 = p1.astype(BF16)
                b2 = p2.astype(BF16)
                delta = (jnp.sum(b1.astype(F32) * d1, axis=1, keepdims=True)
                         + jnp.sum(b2.astype(F32) * d2, axis=1, keepdims=True))
                t1 = (p1 * (d1 - delta)).astype(BF16)
                t2 = (p2 * (d2 - delta)).astype(BF16)
                pscr[rows, :] = b1
                dscr[rows, :] = t1
                kb = k[rows, cols]
                gq[rows, cols] = ((dot_nn(t1, kc) + dot_nn(t2, kb)) * INV).astype(BF16)
                gk[rows, cols] = (dot_tn(t2, q[rows, cols]) * INV).astype(BF16)
                gv[rows, cols] = dot_tn(b2, gb).astype(BF16)
            ck = (dot_tn(dscr[...], q[:, cols]) * INV).astype(BF16)
            cv = dot_tn(pscr[...], ga[:, jc]).astype(BF16)
            for kv, part in ((0, ck), (1, cv)):
                part = part.reshape(NZ, 2, BLOCK, HEAD_DIM)
                for s in range(NZ):
                    for side in range(2):
                        cpart[h, side, s, kv, :, jc] = part[s, side]
            return c

        lax.fori_loop(0, half // HEAD_DIM, head, 0)
        send(rcopy(cpart.at[h, other], crecv.at[h], x_s.at[h], x_r.at[h], partner))

    def pair_sum(h):
        arrived(crecv.at[h], x_r.at[h])

    def cache_sum(h, s):
        return cpart[h, core, s].astype(F32) + crecv[h, s].astype(F32)

    def crs_step(t, h):
        zu = NZ - 1 - t + z
        go_up = jnp.logical_and(zu > z, zu < NZ)
        su = jnp.clip(zu, 0, NZ - 1)
        zl = t - (NZ - 1) + z
        go_dn = jnp.logical_and(zl >= 0, zl < z)
        sl = jnp.clip(zl, 0, NZ - 1)
        for go_, s, got, sems, dev, dst in (
            (go_up, su, has_dn, s_up, up, su),
            (go_dn, sl, has_up, s_dn, dn, jnp.where(zl == z - 1, NZ, sl)),
        ):
            arrived(cbuf.at[h, s], s_rv.at[s, h], jnp.logical_and(go_, got))

            @pl.when(go_)
            def _(s=s):
                cbuf[h, s] = (cbuf[h, s].astype(F32) + cache_sum(h, s)).astype(BF16)

            send(rcopy(cbuf.at[h, s], cbuf.at[h, dst], sems.at[t, h], s_rv.at[dst, h], dev), go_)

    plane_send(1)
    plane_pass(0)
    line_step(1, abuf, a_sems)
    plane_send(2)
    ga_part(0)
    plane_pass(1)
    plane_send(3)
    ga_part(1)
    plane_pass(2)
    line_step(2, abuf, a_sems)
    ga_part(2)
    plane_pass(3)
    ga_part(3)
    for i in range(NZ):
        arrived(grecv.at[zs_of[i]], p_r.at[i])
    rs_step(0, 0)
    rs_step(0, 1)
    line_step(3, abuf, a_sems)
    rs_step(1, 0)
    rs_step(1, 1)
    for s in range(NZ):
        arrived(abuf.at[s, other], a_pr.at[s])
    gw_tile(0)
    rs_step(2, 0)
    gw_tile(1)
    rs_step(2, 1)
    bwd(0)
    pair_sum(0)
    crs_step(0, 0)
    bwd(1)
    crs_step(1, 0)
    pair_sum(1)
    crs_step(0, 1)
    crs_step(2, 0)
    gw_tile(2)
    crs_step(1, 1)
    gw_tile(3)
    crs_step(2, 1)

    for h in range(2):
        arrived(cbuf.at[h, z], s_rv.at[z, h], has_dn)
        arrived(cbuf.at[h, NZ], s_rv.at[NZ, h], has_up)
        gc[:, :, pl.ds(h * half, half)] = (
            cache_sum(h, z) + cbuf[h, z].astype(F32) + cbuf[h, NZ].astype(F32)
        )

    for copy, cond in pending:
        when(cond, copy.wait_send)


def per_device_fused(grad_out, proj_weight, queries, keys, values, cache_keys, cache_values, block_table):
    tok, wid = queries.shape
    half = wid // 2
    dblk = proj_weight.shape[0]
    blocks = tok // BLOCK
    cache = jnp.stack([cache_keys, cache_values])
    named = jnp.any(block_table[:, :, None] == jnp.arange(CB, dtype=jnp.int32), axis=1)
    bias = jnp.repeat(jnp.where(named, 0.0, NEG).astype(F32), BLOCK, axis=1).reshape(blocks, 1, CACHE)
    vm = pl.BlockSpec(memory_space=pltpu.VMEM)
    hbm = pl.BlockSpec(memory_space=pl.ANY)
    dma = pltpu.SemaphoreType.DMA
    out = pl.pallas_call(
        fused_kernel,
        out_shape=(
            jax.ShapeDtypeStruct((tok, wid), BF16),
            jax.ShapeDtypeStruct((tok, wid), BF16),
            jax.ShapeDtypeStruct((tok, wid), BF16),
            jax.ShapeDtypeStruct((2, BLOCK, wid), F32),
            jax.ShapeDtypeStruct((dblk, wid), BF16),
            jax.ShapeDtypeStruct((NZ, 2, BLOCK, dblk), BF16),
            jax.ShapeDtypeStruct((tok, dblk), BF16),
        ),
        in_specs=[hbm, vm, hbm, vm, vm, vm, vm],
        out_specs=[vm] * 5 + [hbm] * 2,
        scratch_shapes=[
            pltpu.VMEM((NZ, 2, 4, BLOCK, dblk), BF16),
            pltpu.VMEM((NZ, 2, 2, BLOCK, wid), BF16),
            pltpu.VMEM((NZ, 2, tok, wid), BF16),
            pltpu.VMEM((2, NZ, 2, tok, half), BF16),
            pltpu.VMEM((NZ, 2, tok, half), BF16),
            pltpu.VMEM((tok, half), BF16),
            pltpu.VMEM((NZ + 1, 2, tok, half), BF16),
            pltpu.VMEM((2, 2, NZ, 2, BLOCK, half), BF16),
            pltpu.VMEM((2, NZ, 2, BLOCK, half), BF16),
            pltpu.VMEM((2, NZ + 1, 2, BLOCK, half), BF16),
            pltpu.VMEM((tok, CACHE), BF16),
            pltpu.VMEM((tok, CACHE), BF16),
            dma((4,)),
            dma((3,)), dma((3,)), dma((NZ,)), dma((7,)), dma((NZ,)),
            dma((3,)), dma((3,)), dma((NZ,)), dma((7,)), dma((NZ,)),
            dma((26,)), dma((26,)),
            dma((NZ,)), dma((NZ,)),
            dma((2,)), dma((2,)),
            dma((3, 2)), dma((3, 2)), dma((NZ + 1, 2)),
            dma((3, 2)), dma((3, 2)), dma((NZ + 1, 2)),
        ],
        compiler_params=pltpu.CompilerParams(
            collective_id=0, has_side_effects=True, vmem_limit_bytes=64 * 1024 * 1024
        ),
        name="fused",
    )(grad_out, proj_weight, cache, queries, keys, values, bias)
    return out[0], out[1], out[2], out[3][0], out[3][1], out[4]


def fits_fused(mesh):
    return mesh.shape["row"] == 4 and mesh.shape["col"] == 2 * NZ


def solution(mesh):
    in_specs = (
        P("col", "row"),
        P("col", "row"),
        P("col", "row"),
        P("col", "row"),
        P("col", "row"),
        P("col", "row"),
        P("col", "row"),
        P("col", None),
    )
    out_specs = (
        P("col", "row"),
        P("col", "row"),
        P("col", "row"),
        P("col", "row"),
        P("col", "row"),
        P("col", "row"),
    )
    return jax.shard_map(
        per_device_fused if fits_fused(mesh) else per_device, mesh=mesh, in_specs=in_specs, out_specs=out_specs, check_vma=False
    )
```

```python
import math

import jax
import jax.numpy as jnp
from jax import lax
from jax.experimental import pallas as pl
from jax.experimental.pallas import tpu as pltpu
from jax.sharding import PartitionSpec as P

HEAD_DIM = 128
BLOCK = 128
CB = 8
KB = 4
CACHE = 1024


def per_device(grad_out, proj_weight, queries, keys, values, cache_keys, cache_values, block_table):
    tok_rows = grad_out.shape[0]
    local_width = queries.shape[1]
    head_count = local_width // HEAD_DIM
    inverse_root = 1.0 / math.sqrt(HEAD_DIM)
    full_grads = lax.all_gather(grad_out, "row", axis=1, tiled=True)
    columns = full_grads
    grad_sum = jnp.dot(
        columns,
        lax.all_gather(proj_weight, "col", axis=0, tiled=True),
        preferred_element_type=jnp.float32,
    )
    grad_attn = grad_sum.astype(jnp.bfloat16)
    cache_k_all, cache_v_all = (
        lax.all_gather(cache_keys, "col", axis=0, tiled=True),
        lax.all_gather(cache_values, "col", axis=0, tiled=True),
    )
    cache_key_blocks = cache_k_all.reshape(CB, BLOCK, head_count, HEAD_DIM)
    cache_value_blocks = cache_v_all.reshape(CB, BLOCK, head_count, HEAD_DIM)
    blocks_here = tok_rows // BLOCK
    group = math.gcd(blocks_here, max(1, 512 // BLOCK))
    turns = blocks_here // group
    positions = jnp.arange(BLOCK, dtype=jnp.int32)
    causal = positions[:, None] >= positions[None, :]
    allowed = jnp.concatenate([jnp.ones((BLOCK, KB * BLOCK), dtype=bool), causal], axis=1)
    block_ids = jnp.arange(CB, dtype=jnp.int32)

    def to_groups(array):
        return array.reshape(turns, group, BLOCK, head_count, HEAD_DIM)

    def one_group(carry, inputs):
        grad_ck, grad_cv = carry
        query, own_keys, own_values, grad_block, chosen = inputs
        picked_keys = cache_key_blocks[chosen].reshape(group, KB * BLOCK, head_count, HEAD_DIM)
        picked_values = cache_value_blocks[chosen].reshape(group, KB * BLOCK, head_count, HEAD_DIM)
        key_list = jnp.concatenate([picked_keys, own_keys], axis=1)
        value_list = jnp.concatenate([picked_values, own_values], axis=1)
        scores = (
            jnp.einsum("gqhd,gkhd->ghqk", query, key_list, preferred_element_type=jnp.float32)
            * inverse_root
        )
        scores = jnp.where(allowed[None, None], scores, -jnp.inf)
        row_max = jnp.max(scores, axis=-1, keepdims=True)
        weights = jnp.exp(scores - row_max)
        probs = weights / jnp.sum(weights, axis=-1, keepdims=True)
        probs_b = probs.astype(jnp.bfloat16)
        attn_full = jnp.einsum(
            "ghqk,gkhd->gqhd", probs_b, value_list, preferred_element_type=jnp.float32
        )
        grad_probs = jnp.einsum(
            "gqhd,gkhd->ghqk", grad_block, value_list, preferred_element_type=jnp.float32
        )
        delta = jnp.sum(grad_block.astype(jnp.float32) * attn_full, axis=-1)
        delta = jnp.transpose(delta, (0, 2, 1))[..., None]
        grad_scores = (probs * (grad_probs - delta)).astype(jnp.bfloat16)
        grad_query = (
            jnp.einsum("ghqk,gkhd->gqhd", grad_scores, key_list, preferred_element_type=jnp.float32)
            * inverse_root
        )
        grad_key_list = (
            jnp.einsum("ghqk,gqhd->gkhd", grad_scores, query, preferred_element_type=jnp.float32)
            * inverse_root
        )
        grad_value_list = jnp.einsum(
            "ghqk,gqhd->gkhd", probs_b, grad_block, preferred_element_type=jnp.float32
        )
        one_hot = (chosen.reshape(group * KB)[:, None] == block_ids[None, :]).astype(jnp.float32)
        cache_key_part = grad_key_list[:, : KB * BLOCK].reshape(group * KB, BLOCK * local_width)
        cache_value_part = grad_value_list[:, : KB * BLOCK].reshape(group * KB, BLOCK * local_width)
        grad_ck = grad_ck + jnp.dot(one_hot.T, cache_key_part, precision=lax.Precision.HIGHEST)
        grad_cv = grad_cv + jnp.dot(one_hot.T, cache_value_part, precision=lax.Precision.HIGHEST)
        outputs = (
            grad_query.astype(jnp.bfloat16),
            grad_key_list[:, KB * BLOCK :].astype(jnp.bfloat16),
            grad_value_list[:, KB * BLOCK :].astype(jnp.bfloat16),
            attn_full.astype(jnp.bfloat16),
        )
        return ((grad_ck, grad_cv), outputs)

    start_carry = (
        jnp.zeros((CB, BLOCK * local_width), jnp.float32),
        jnp.zeros((CB, BLOCK * local_width), jnp.float32),
    )
    inputs = (
        to_groups(queries),
        to_groups(keys),
        to_groups(values),
        to_groups(grad_attn),
        block_table.reshape(turns, group, KB),
    )
    (grad_ck, grad_cv), outputs = lax.scan(one_group, start_carry, inputs)
    grad_q = outputs[0].reshape(tok_rows, local_width)
    grad_k = outputs[1].reshape(tok_rows, local_width)
    grad_v = outputs[2].reshape(tok_rows, local_width)
    attn_out = outputs[3].reshape(tok_rows, local_width)
    grad_cache_k, grad_cache_v = (
        lax.psum_scatter(
            grad_ck.reshape(CACHE, local_width).astype(jnp.bfloat16),
            "col",
            scatter_dimension=0,
            tiled=True,
        ).astype(jnp.float32),
        lax.psum_scatter(
            grad_cv.reshape(CACHE, local_width).astype(jnp.bfloat16),
            "col",
            scatter_dimension=0,
            tiled=True,
        ).astype(jnp.float32),
    )
    columns = full_grads
    grad_weight = lax.psum_scatter(
        lax.dot_general(
            columns, attn_out, (((0,), (0,)), ((), ())), preferred_element_type=jnp.float32
        ).astype(jnp.bfloat16),
        "col",
        scatter_dimension=0,
        tiled=True,
    )
    return (grad_q, grad_k, grad_v, grad_cache_k, grad_cache_v, grad_weight)


F32 = jnp.float32
BF16 = jnp.bfloat16
INV = 1.0 / math.sqrt(HEAD_DIM)
NZ = 4
NEG = -1e30
INV2 = INV * math.log2(math.e)


def dot_nt(a, b):
    return lax.dot_general(a, b, (((1,), (1,)), ((), ())), preferred_element_type=F32)


def dot_tn(a, b):
    return lax.dot_general(a, b, (((0,), (0,)), ((), ())), preferred_element_type=F32)


def dot_nn(a, b):
    return jnp.dot(a, b, preferred_element_type=F32)


def fused_kernel(
    go, w, cache, q, k, v, tz, tc, slot_of,
    gq, gk, gv, gck, gcv, gw, H, gx,
    G, ckv, abuf, gpart, grecv, ga, rbuf, cpart, crecv, cbuf, pscr, dscr, lse,
    loc_sem, c_up, c_dn, c_rv, c_ps, c_pr, a_up, a_dn, a_rv, a_ps, a_pr,
    g_s, g_r, p_s, p_r, x_s, x_r, r_up, r_dn, r_rv, s_up, s_dn, s_rv,
):
    col = lax.axis_index("col")
    row = lax.axis_index("row")
    z = col // 2
    core = col % 2
    other = 1 - core
    has_up = z < NZ - 1
    has_dn = z > 0
    partner = {"col": z * 2 + other}
    up = {"col": jnp.minimum(col + 2, 2 * NZ - 2 + core)}
    dn = {"col": jnp.maximum(col - 2, core)}
    rx = row + 1 - 2 * (row % 2)
    ry = (row + 2) % 4
    rd = (rx + 2) % 4
    xn = {"row": rx}
    yn = {"row": ry}
    dg = {"row": rd}
    tok = q.shape[0]
    wid = q.shape[1]
    half = wid // 2
    dblk = w.shape[0]
    pending = []

    def rcopy(src, dst, ss, rs, dev):
        return pltpu.make_async_remote_copy(
            src_ref=src, dst_ref=dst, send_sem=ss, recv_sem=rs,
            device_id=dev, device_id_type=pl.DeviceIdType.MESH,
        )

    def when(cond, fn):
        if cond is None:
            fn()
        else:
            pl.when(cond)(fn)

    def send(copy, cond=None):
        when(cond, copy.start)
        pending.append((copy, cond))

    def arrived(ref, sem, cond=None):
        when(cond, lambda: pltpu.make_async_copy(ref, ref, sem).wait())

    barrier = pltpu.get_barrier_semaphore()

    def greet(dev):
        pl.semaphore_signal(barrier, inc=1, device_id=dev, device_id_type=pl.DeviceIdType.MESH)

    zs_of = [(z + NZ - i) % NZ for i in range(NZ)]
    zd_of = [(z + i) % NZ for i in range(NZ)]
    line = [{"col": zd_of[i] * 2 + core} for i in range(NZ)]
    for dev in (partner, xn, yn, dg, line[1], line[2], line[3]):
        greet(dev)
    pl.semaphore_wait(barrier, 7)

    def line_own(src, buf, sems):
        s_u, s_d, rv, ps, pr = sems
        send(rcopy(src, buf.at[z, core], s_u.at[0], rv.at[z], up), has_up)
        send(rcopy(src, buf.at[z, core], s_d.at[0], rv.at[z], dn), has_dn)
        send(rcopy(src, buf.at[z, core], ps.at[0], pr.at[z], partner))

    def line_step(t, buf, sems):
        s_u, s_d, rv, ps, pr = sems
        below, above = z - t, z + t
        lo, hi = jnp.maximum(below, 0), jnp.minimum(above, NZ - 1)
        got_lo, got_hi = below >= 0, above < NZ
        for s, got, hop, ss, dev, n in (
            (lo, got_lo, has_up, s_u, up, 2 * t - 1),
            (hi, got_hi, has_dn, s_d, dn, 2 * t),
        ):
            piece = buf.at[s, core]
            arrived(piece, rv.at[s], got)
            if t < NZ - 1:
                send(rcopy(piece, piece, ss.at[t], rv.at[s], dev), jnp.logical_and(got, hop))
            send(rcopy(piece, piece, ps.at[n], pr.at[s], partner), got)

    c_sems = (c_up, c_dn, c_rv, c_ps, c_pr)
    a_sems = (a_up, a_dn, a_rv, a_ps, a_pr)
    line_own(cache, ckv, c_sems)
    mine = pl.ds(pl.multiple_of(core * dblk, dblk), dblk)
    theirs = pl.ds(pl.multiple_of(other * dblk, dblk), dblk)
    send(rcopy(go.at[:, theirs], gx, g_s.at[0], g_r.at[0], partner))

    def quarter(r):
        return pl.ds(pl.multiple_of(r * BLOCK, BLOCK), BLOCK)

    plane = ((rx, xn), (ry, yn), (rd, dg))
    for n, (r, dev) in enumerate(plane):
        send(rcopy(go.at[quarter(r), mine], H.at[row, core], g_s.at[1 + n], g_r.at[1 + 2 * n + core], dev))

    locals_ = [
        pltpu.make_async_copy(cache, ckv.at[z, core], loc_sem.at[0]),
        pltpu.make_async_copy(go.at[quarter(row), mine], H.at[row, core], loc_sem.at[1]),
    ]
    for c in locals_:
        c.start()

    def clear(s):
        rbuf[s] = jnp.zeros(rbuf.shape[1:], BF16)
        for h in range(2):
            cbuf[h, s] = jnp.zeros(cbuf.shape[2:], BF16)

    @pl.when(z == 0)
    def _():
        lax.fori_loop(0, NZ, lambda s, c: (clear(s), c)[1], 0)

    @pl.when(z == NZ - 1)
    def _():
        lax.fori_loop(0, NZ - 1, lambda s, c: (clear(s), c)[1], 0)
        clear(NZ)

    line_step(1, ckv, c_sems)
    arrived(gx, g_r.at[0])
    for n, (r, dev) in enumerate(plane):
        send(rcopy(gx.at[quarter(r)], H.at[row, other], g_s.at[4 + n], g_r.at[1 + 2 * n + other], dev))
    own_gx = pltpu.make_async_copy(gx.at[quarter(row)], H.at[row, other], loc_sem.at[2])
    own_gx.start()
    line_step(2, ckv, c_sems)
    for c in locals_:
        c.wait()
    own_gx.wait()
    for n, (r, dev) in enumerate(plane):
        for side in range(2):
            arrived(H.at[r, side], g_r.at[1 + 2 * n + side])
    own_h = pltpu.make_async_copy(H.at[z], G.at[z, :, row], loc_sem.at[3])
    own_h.start()
    for i in range(1, NZ):
        send(rcopy(H.at[zd_of[i]], G.at[z, :, row], g_s.at[6 + i], g_r.at[6 + i], line[i]))

    def plane_send(i):
        piece = G.at[zs_of[i], :, row]
        if i == 0:
            own_h.wait()
        else:
            arrived(piece, g_r.at[6 + i])
        send(rcopy(piece, piece, g_s.at[10 + i], g_r.at[10 + i], xn))
        send(rcopy(piece, piece, g_s.at[14 + i], g_r.at[14 + i], yn))

    def plane_pass(i):
        zs = zs_of[i]
        arrived(G.at[zs, :, rx], g_r.at[10 + i])
        send(rcopy(G.at[zs, 0, rx], G.at[zs, 0, rx], g_s.at[18 + i], g_r.at[18 + i], yn))
        arrived(G.at[zs, :, ry], g_r.at[14 + i])
        send(rcopy(G.at[zs, 1, ry], G.at[zs, 1, ry], g_s.at[22 + i], g_r.at[22 + i], xn))

    plane_send(0)
    line_step(3, ckv, c_sems)
    for s in range(NZ):
        arrived(ckv.at[s, other], c_pr.at[s])

    causal = (lax.broadcasted_iota(jnp.int32, (BLOCK, BLOCK), 0)
              >= lax.broadcasted_iota(jnp.int32, (BLOCK, BLOCK), 1))
    blocks = tok // BLOCK

    def head_cols(h):
        return pl.ds(pl.multiple_of(h * HEAD_DIM, HEAD_DIM), HEAD_DIM)

    def listed(kv, b, cols):
        return jnp.concatenate([ckv[tz[b, j], tc[b, j], kv, :, cols] for j in range(KB)], axis=0)

    def scores_of(rows, cols, kc):
        qb = q[rows, cols]
        s1 = dot_nt(qb, kc) * INV2
        s2 = jnp.where(causal, dot_nt(qb, k[rows, cols]) * INV2, NEG)
        return s1, s2

    def fwd_head(h, c):
        cols = head_cols(h)
        for b in range(blocks):
            rows = pl.ds(b * BLOCK, BLOCK)
            s1, s2 = scores_of(rows, cols, listed(0, b, cols))
            m = jnp.maximum(jnp.max(s1, axis=1, keepdims=True), jnp.max(s2, axis=1, keepdims=True))
            e1 = jnp.exp2(s1 - m)
            e2 = jnp.exp2(s2 - m)
            total = jnp.sum(e1, axis=1, keepdims=True) + jnp.sum(e2, axis=1, keepdims=True)
            o = dot_nn(e1.astype(BF16), listed(1, b, cols)) + dot_nn(e2.astype(BF16), v[rows, cols])
            abuf[z, core, rows, cols] = (o / total).astype(BF16)
            lse[h, rows, :] = m + jnp.log2(total)
        return c

    for b in range(blocks):
        pscr[b, KB] = jnp.zeros((BLOCK, BLOCK), BF16)
        dscr[b, KB] = jnp.zeros((BLOCK, BLOCK), BF16)
    lax.fori_loop(0, wid // HEAD_DIM, fwd_head, 0)
    line_own(abuf.at[z, core], abuf, a_sems)

    tile = 256

    def ga_part(i):
        zs = zs_of[i]
        arrived(G.at[zs, 0, rd], g_r.at[18 + i])
        arrived(G.at[zs, 1, rd], g_r.at[22 + i])

        def body(n, c):
            side = n // 2
            part = n % 2
            rows = pl.ds(pl.multiple_of(part * tile, tile), tile)
            lhs = G[zs, side, pl.ds(part * 2, 2)].reshape(tile, dblk)
            for h in range(2):
                acc = dot_nn(lhs, w[:, pl.ds(h * half, half)])
                gpart[side, zs, h, rows, :] = acc.astype(BF16)
            return c

        lax.fori_loop(0, 4, body, 0)
        send(rcopy(gpart.at[other, zs], grecv.at[zs], p_s.at[i], p_r.at[i], partner))

    def gw_tile(n):
        rows = pl.ds(n * tile, tile)
        acc = None
        for s in range(NZ):
            lhs = G[s, :, :, :, rows].reshape(2 * tok, tile)
            part = dot_tn(lhs, abuf[s].reshape(2 * tok, wid))
            acc = part if acc is None else acc + part
        gw[rows, :] = acc.astype(BF16)

    def ga_sum(s, h, rows):
        return (gpart[core, s, h, rows, :].astype(F32) + grecv[s, h, rows, :].astype(F32)
                + rbuf[s, h, rows, :].astype(F32))

    def rs_step(t, h):
        zu = NZ - 1 - t + z
        go_up = jnp.logical_and(zu > z, zu < NZ)
        su = jnp.clip(zu, 0, NZ - 1)
        zl = t - (NZ - 1) + z
        go_dn = jnp.logical_and(zl >= 0, zl < z)
        sl = jnp.clip(zl, 0, NZ - 1)
        for go_, s, got, sems, dev, dst in (
            (go_up, su, has_dn, r_up, up, su),
            (go_dn, sl, has_up, r_dn, dn, jnp.where(zl == z - 1, NZ, sl)),
        ):
            arrived(rbuf.at[s, h], r_rv.at[s, h], jnp.logical_and(go_, got))

            @pl.when(go_)
            def _(s=s):
                def body(n, c):
                    rows = pl.ds(pl.multiple_of(n * BLOCK, BLOCK), BLOCK)
                    rbuf[s, h, rows, :] = ga_sum(s, h, rows).astype(BF16)
                    return c
                lax.fori_loop(0, tok // BLOCK, body, 0)

            send(rcopy(rbuf.at[s, h], rbuf.at[dst, h], sems.at[t, h], r_rv.at[dst, h], dev), go_)

    def bwd(h):
        arrived(rbuf.at[z, h], r_rv.at[z, h], has_dn)
        arrived(rbuf.at[NZ, h], r_rv.at[NZ, h], has_up)

        def total(n, c):
            rows = pl.ds(pl.multiple_of(n * BLOCK, BLOCK), BLOCK)
            ga[rows, :] = (ga_sum(z, h, rows) + rbuf[NZ, h, rows, :].astype(F32)).astype(BF16)
            return c

        lax.fori_loop(0, blocks, total, 0)

        def head(j, c):
            hd = h * (half // HEAD_DIM) + j
            cols = head_cols(hd)
            jc = head_cols(j)
            for b in range(blocks):
                rows = pl.ds(b * BLOCK, BLOCK)
                kc = listed(0, b, cols)
                s1, s2 = scores_of(rows, cols, kc)
                norm = lse[hd, rows, :]
                p1 = jnp.exp2(s1 - norm)
                p2 = jnp.exp2(s2 - norm)
                gb = ga[rows, jc]
                d1 = dot_nt(gb, listed(1, b, cols))
                d2 = dot_nt(gb, v[rows, cols])
                delta = jnp.sum(gb.astype(F32) * abuf[z, core, rows, cols].astype(F32), axis=1, keepdims=True)
                b1 = p1.astype(BF16)
                b2 = p2.astype(BF16)
                t1 = (p1 * (d1 - delta)).astype(BF16)
                t2 = (p2 * (d2 - delta)).astype(BF16)
                for n in range(KB):
                    pscr[b, n] = b1[:, n * BLOCK : (n + 1) * BLOCK]
                    dscr[b, n] = t1[:, n * BLOCK : (n + 1) * BLOCK]
                kb = k[rows, cols]
                gq[rows, cols] = ((dot_nn(t1, kc) + dot_nn(t2, kb)) * INV).astype(BF16)
                gk[rows, cols] = (dot_tn(t2, q[rows, cols]) * INV).astype(BF16)
                gv[rows, cols] = dot_tn(b2, gb).astype(BF16)
            qh = q[:, cols]
            gh = ga[:, jc]
            for s in range(NZ):
                for side in range(2):
                    ds = jnp.concatenate([dscr[b, slot_of[b, 2 * s + side]] for b in range(blocks)], axis=0)
                    ps = jnp.concatenate([pscr[b, slot_of[b, 2 * s + side]] for b in range(blocks)], axis=0)
                    cpart[h, side, s, 0, :, jc] = (dot_tn(ds, qh) * INV).astype(BF16)
                    cpart[h, side, s, 1, :, jc] = dot_tn(ps, gh).astype(BF16)
            return c

        lax.fori_loop(0, half // HEAD_DIM, head, 0)
        send(rcopy(cpart.at[h, other], crecv.at[h], x_s.at[h], x_r.at[h], partner))

    def pair_sum(h):
        arrived(crecv.at[h], x_r.at[h])

    def cache_sum(h, s):
        return cpart[h, core, s].astype(F32) + crecv[h, s].astype(F32)

    def crs_step(t, h):
        zu = NZ - 1 - t + z
        go_up = jnp.logical_and(zu > z, zu < NZ)
        su = jnp.clip(zu, 0, NZ - 1)
        zl = t - (NZ - 1) + z
        go_dn = jnp.logical_and(zl >= 0, zl < z)
        sl = jnp.clip(zl, 0, NZ - 1)
        for go_, s, got, sems, dev, dst in (
            (go_up, su, has_dn, s_up, up, su),
            (go_dn, sl, has_up, s_dn, dn, jnp.where(zl == z - 1, NZ, sl)),
        ):
            arrived(cbuf.at[h, s], s_rv.at[s, h], jnp.logical_and(go_, got))

            @pl.when(go_)
            def _(s=s):
                cbuf[h, s] = (cbuf[h, s].astype(F32) + cache_sum(h, s)).astype(BF16)

            send(rcopy(cbuf.at[h, s], cbuf.at[h, dst], sems.at[t, h], s_rv.at[dst, h], dev), go_)

    plane_send(1)
    plane_pass(0)
    line_step(1, abuf, a_sems)
    plane_send(2)
    ga_part(0)
    plane_pass(1)
    plane_send(3)
    ga_part(1)
    plane_pass(2)
    line_step(2, abuf, a_sems)
    ga_part(2)
    plane_pass(3)
    ga_part(3)
    for i in range(NZ):
        arrived(grecv.at[zs_of[i]], p_r.at[i])
    rs_step(0, 0)
    rs_step(0, 1)
    line_step(3, abuf, a_sems)
    rs_step(1, 0)
    rs_step(1, 1)
    for s in range(NZ):
        arrived(abuf.at[s, other], a_pr.at[s])
    gw_tile(0)
    rs_step(2, 0)
    gw_tile(1)
    rs_step(2, 1)
    bwd(0)
    pair_sum(0)
    crs_step(0, 0)
    bwd(1)
    crs_step(1, 0)
    pair_sum(1)
    crs_step(0, 1)
    crs_step(2, 0)
    gw_tile(2)
    crs_step(1, 1)
    gw_tile(3)
    crs_step(2, 1)

    for h in range(2):
        arrived(cbuf.at[h, z], s_rv.at[z, h], has_dn)
        arrived(cbuf.at[h, NZ], s_rv.at[NZ, h], has_up)
        total = cache_sum(h, z) + cbuf[h, z].astype(F32) + cbuf[h, NZ].astype(F32)
        gck[:, pl.ds(h * half, half)] = total[0]
        gcv[:, pl.ds(h * half, half)] = total[1]

    for copy, cond in pending:
        when(cond, copy.wait_send)


def per_device_fused(grad_out, proj_weight, queries, keys, values, cache_keys, cache_values, block_table):
    tok, wid = queries.shape
    half = wid // 2
    dblk = proj_weight.shape[0]
    blocks = tok // BLOCK
    cache = jnp.stack([cache_keys, cache_values])
    match = block_table[:, :, None] == jnp.arange(CB, dtype=jnp.int32)
    slot_of = KB - jnp.sum(match * (KB - jnp.arange(KB, dtype=jnp.int32))[None, :, None], axis=1)
    sm = pl.BlockSpec(memory_space=pltpu.SMEM)
    vm = pl.BlockSpec(memory_space=pltpu.VMEM)
    hbm = pl.BlockSpec(memory_space=pl.ANY)
    dma = pltpu.SemaphoreType.DMA
    out = pl.pallas_call(
        fused_kernel,
        out_shape=(
            jax.ShapeDtypeStruct((tok, wid), BF16),
            jax.ShapeDtypeStruct((tok, wid), BF16),
            jax.ShapeDtypeStruct((tok, wid), BF16),
            jax.ShapeDtypeStruct((BLOCK, wid), F32),
            jax.ShapeDtypeStruct((BLOCK, wid), F32),
            jax.ShapeDtypeStruct((dblk, wid), BF16),
            jax.ShapeDtypeStruct((NZ, 2, BLOCK, dblk), BF16),
            jax.ShapeDtypeStruct((tok, dblk), BF16),
        ),
        in_specs=[hbm, vm, hbm, vm, vm, vm, sm, sm, sm],
        out_specs=[vm] * 6 + [hbm] * 2,
        scratch_shapes=[
            pltpu.VMEM((NZ, 2, 4, BLOCK, dblk), BF16),
            pltpu.VMEM((NZ, 2, 2, BLOCK, wid), BF16),
            pltpu.VMEM((NZ, 2, tok, wid), BF16),
            pltpu.VMEM((2, NZ, 2, tok, half), BF16),
            pltpu.VMEM((NZ, 2, tok, half), BF16),
            pltpu.VMEM((tok, half), BF16),
            pltpu.VMEM((NZ + 1, 2, tok, half), BF16),
            pltpu.VMEM((2, 2, NZ, 2, BLOCK, half), BF16),
            pltpu.VMEM((2, NZ, 2, BLOCK, half), BF16),
            pltpu.VMEM((2, NZ + 1, 2, BLOCK, half), BF16),
            pltpu.VMEM((blocks, KB + 1, BLOCK, BLOCK), BF16),
            pltpu.VMEM((blocks, KB + 1, BLOCK, BLOCK), BF16),
            pltpu.VMEM((wid // HEAD_DIM, tok, 1), F32),
            dma((4,)),
            dma((3,)), dma((3,)), dma((NZ,)), dma((7,)), dma((NZ,)),
            dma((3,)), dma((3,)), dma((NZ,)), dma((7,)), dma((NZ,)),
            dma((26,)), dma((26,)),
            dma((NZ,)), dma((NZ,)),
            dma((2,)), dma((2,)),
            dma((3, 2)), dma((3, 2)), dma((NZ + 1, 2)),
            dma((3, 2)), dma((3, 2)), dma((NZ + 1, 2)),
        ],
        compiler_params=pltpu.CompilerParams(
            collective_id=0, has_side_effects=True, vmem_limit_bytes=64 * 1024 * 1024
        ),
        name="fused",
    )(grad_out, proj_weight, cache, queries, keys, values, block_table // 2, block_table % 2, slot_of)
    return out[:6]


def fits_fused(mesh):
    return mesh.shape["row"] == 4 and mesh.shape["col"] == 2 * NZ


def solution(mesh):
    in_specs = (
        P("col", "row"),
        P("col", "row"),
        P("col", "row"),
        P("col", "row"),
        P("col", "row"),
        P("col", "row"),
        P("col", "row"),
        P("col", None),
    )
    out_specs = (
        P("col", "row"),
        P("col", "row"),
        P("col", "row"),
        P("col", "row"),
        P("col", "row"),
        P("col", "row"),
    )
    return jax.shard_map(
        per_device_fused if fits_fused(mesh) else per_device, mesh=mesh, in_specs=in_specs, out_specs=out_specs, check_vma=False
    )
```

```python
import math

import jax
import jax.numpy as jnp
from jax import lax
from jax.experimental import pallas as pl
from jax.experimental.pallas import tpu as pltpu
from jax.sharding import PartitionSpec as P

HEAD_DIM = 128
BLOCK = 128
CB = 8
KB = 4
CACHE = 1024


def per_device(grad_out, proj_weight, queries, keys, values, cache_keys, cache_values, block_table):
    tok_rows = grad_out.shape[0]
    local_width = queries.shape[1]
    head_count = local_width // HEAD_DIM
    inverse_root = 1.0 / math.sqrt(HEAD_DIM)
    full_grads = lax.all_gather(grad_out, "row", axis=1, tiled=True)
    columns = full_grads
    grad_sum = jnp.dot(
        columns,
        lax.all_gather(proj_weight, "col", axis=0, tiled=True),
        preferred_element_type=jnp.float32,
    )
    grad_attn = grad_sum.astype(jnp.bfloat16)
    cache_k_all, cache_v_all = (
        lax.all_gather(cache_keys, "col", axis=0, tiled=True),
        lax.all_gather(cache_values, "col", axis=0, tiled=True),
    )
    cache_key_blocks = cache_k_all.reshape(CB, BLOCK, head_count, HEAD_DIM)
    cache_value_blocks = cache_v_all.reshape(CB, BLOCK, head_count, HEAD_DIM)
    blocks_here = tok_rows // BLOCK
    group = math.gcd(blocks_here, max(1, 512 // BLOCK))
    turns = blocks_here // group
    positions = jnp.arange(BLOCK, dtype=jnp.int32)
    causal = positions[:, None] >= positions[None, :]
    allowed = jnp.concatenate([jnp.ones((BLOCK, KB * BLOCK), dtype=bool), causal], axis=1)
    block_ids = jnp.arange(CB, dtype=jnp.int32)

    def to_groups(array):
        return array.reshape(turns, group, BLOCK, head_count, HEAD_DIM)

    def one_group(carry, inputs):
        grad_ck, grad_cv = carry
        query, own_keys, own_values, grad_block, chosen = inputs
        picked_keys = cache_key_blocks[chosen].reshape(group, KB * BLOCK, head_count, HEAD_DIM)
        picked_values = cache_value_blocks[chosen].reshape(group, KB * BLOCK, head_count, HEAD_DIM)
        key_list = jnp.concatenate([picked_keys, own_keys], axis=1)
        value_list = jnp.concatenate([picked_values, own_values], axis=1)
        scores = (
            jnp.einsum("gqhd,gkhd->ghqk", query, key_list, preferred_element_type=jnp.float32)
            * inverse_root
        )
        scores = jnp.where(allowed[None, None], scores, -jnp.inf)
        row_max = jnp.max(scores, axis=-1, keepdims=True)
        weights = jnp.exp(scores - row_max)
        probs = weights / jnp.sum(weights, axis=-1, keepdims=True)
        probs_b = probs.astype(jnp.bfloat16)
        attn_full = jnp.einsum(
            "ghqk,gkhd->gqhd", probs_b, value_list, preferred_element_type=jnp.float32
        )
        grad_probs = jnp.einsum(
            "gqhd,gkhd->ghqk", grad_block, value_list, preferred_element_type=jnp.float32
        )
        delta = jnp.sum(grad_block.astype(jnp.float32) * attn_full, axis=-1)
        delta = jnp.transpose(delta, (0, 2, 1))[..., None]
        grad_scores = (probs * (grad_probs - delta)).astype(jnp.bfloat16)
        grad_query = (
            jnp.einsum("ghqk,gkhd->gqhd", grad_scores, key_list, preferred_element_type=jnp.float32)
            * inverse_root
        )
        grad_key_list = (
            jnp.einsum("ghqk,gqhd->gkhd", grad_scores, query, preferred_element_type=jnp.float32)
            * inverse_root
        )
        grad_value_list = jnp.einsum(
            "ghqk,gqhd->gkhd", probs_b, grad_block, preferred_element_type=jnp.float32
        )
        one_hot = (chosen.reshape(group * KB)[:, None] == block_ids[None, :]).astype(jnp.float32)
        cache_key_part = grad_key_list[:, : KB * BLOCK].reshape(group * KB, BLOCK * local_width)
        cache_value_part = grad_value_list[:, : KB * BLOCK].reshape(group * KB, BLOCK * local_width)
        grad_ck = grad_ck + jnp.dot(one_hot.T, cache_key_part, precision=lax.Precision.HIGHEST)
        grad_cv = grad_cv + jnp.dot(one_hot.T, cache_value_part, precision=lax.Precision.HIGHEST)
        outputs = (
            grad_query.astype(jnp.bfloat16),
            grad_key_list[:, KB * BLOCK :].astype(jnp.bfloat16),
            grad_value_list[:, KB * BLOCK :].astype(jnp.bfloat16),
            attn_full.astype(jnp.bfloat16),
        )
        return ((grad_ck, grad_cv), outputs)

    start_carry = (
        jnp.zeros((CB, BLOCK * local_width), jnp.float32),
        jnp.zeros((CB, BLOCK * local_width), jnp.float32),
    )
    inputs = (
        to_groups(queries),
        to_groups(keys),
        to_groups(values),
        to_groups(grad_attn),
        block_table.reshape(turns, group, KB),
    )
    (grad_ck, grad_cv), outputs = lax.scan(one_group, start_carry, inputs)
    grad_q = outputs[0].reshape(tok_rows, local_width)
    grad_k = outputs[1].reshape(tok_rows, local_width)
    grad_v = outputs[2].reshape(tok_rows, local_width)
    attn_out = outputs[3].reshape(tok_rows, local_width)
    grad_cache_k, grad_cache_v = (
        lax.psum_scatter(
            grad_ck.reshape(CACHE, local_width).astype(jnp.bfloat16),
            "col",
            scatter_dimension=0,
            tiled=True,
        ).astype(jnp.float32),
        lax.psum_scatter(
            grad_cv.reshape(CACHE, local_width).astype(jnp.bfloat16),
            "col",
            scatter_dimension=0,
            tiled=True,
        ).astype(jnp.float32),
    )
    columns = full_grads
    grad_weight = lax.psum_scatter(
        lax.dot_general(
            columns, attn_out, (((0,), (0,)), ((), ())), preferred_element_type=jnp.float32
        ).astype(jnp.bfloat16),
        "col",
        scatter_dimension=0,
        tiled=True,
    )
    return (grad_q, grad_k, grad_v, grad_cache_k, grad_cache_v, grad_weight)


F32 = jnp.float32
BF16 = jnp.bfloat16
INV = 1.0 / math.sqrt(HEAD_DIM)
NZ = 4
NEG = -1e30
INV2 = INV * math.log2(math.e)


def dot_nt(a, b):
    return lax.dot_general(a, b, (((1,), (1,)), ((), ())), preferred_element_type=F32)


def dot_tn(a, b):
    return lax.dot_general(a, b, (((0,), (0,)), ((), ())), preferred_element_type=F32)


def dot_nn(a, b):
    return jnp.dot(a, b, preferred_element_type=F32)


def fused_kernel(
    go, w, cache, q, k, v, tz, tc, slot_of,
    gq, gk, gv, gck, gcv, gw, H, gx,
    G, ckv, abuf, gpart, grecv, ga, rbuf, cpart, crecv, cbuf, pscr, dscr, lse,
    loc_sem, c_up, c_dn, c_rv, c_ps, c_pr, a_up, a_dn, a_rv, a_ps, a_pr,
    g_s, g_r, p_s, p_r, x_s, x_r, r_up, r_dn, r_rv, s_up, s_dn, s_rv,
):
    col = lax.axis_index("col")
    row = lax.axis_index("row")
    z = col // 2
    core = col % 2
    other = 1 - core
    has_up = z < NZ - 1
    has_dn = z > 0
    partner = {"col": z * 2 + other}
    up = {"col": jnp.minimum(col + 2, 2 * NZ - 2 + core)}
    dn = {"col": jnp.maximum(col - 2, core)}
    rx = row + 1 - 2 * (row % 2)
    ry = (row + 2) % 4
    rd = (rx + 2) % 4
    xn = {"row": rx}
    yn = {"row": ry}
    dg = {"row": rd}
    tok = q.shape[0]
    wid = q.shape[1]
    half = wid // 2
    dblk = w.shape[0]
    pending = []

    def rcopy(src, dst, ss, rs, dev):
        return pltpu.make_async_remote_copy(
            src_ref=src, dst_ref=dst, send_sem=ss, recv_sem=rs,
            device_id=dev, device_id_type=pl.DeviceIdType.MESH,
        )

    def when(cond, fn):
        if cond is None:
            fn()
        else:
            pl.when(cond)(fn)

    def send(copy, cond=None):
        when(cond, copy.start)
        pending.append((copy, cond))

    def arrived(ref, sem, cond=None):
        when(cond, lambda: pltpu.make_async_copy(ref, ref, sem).wait())

    barrier = pltpu.get_barrier_semaphore()

    def greet(dev):
        pl.semaphore_signal(barrier, inc=1, device_id=dev, device_id_type=pl.DeviceIdType.MESH)

    zs_of = [z]
    for i in range(1, NZ):
        high = jnp.where(NZ - i > z, NZ - i, NZ - i - 1)
        low = jnp.where(i - 1 < z, i - 1, i)
        zs_of.append(jnp.where(z < NZ // 2, high, low))
    zd_of = [(z + i) % NZ for i in range(NZ)]
    line = [{"col": zd_of[i] * 2 + core} for i in range(NZ)]
    for dev in (partner, xn, yn, dg, line[1], line[2], line[3]):
        greet(dev)
    pl.semaphore_wait(barrier, 7)

    def line_own(src, buf, sems):
        s_u, s_d, rv, ps, pr = sems
        send(rcopy(src, buf.at[z, core], s_u.at[0], rv.at[z], up), has_up)
        send(rcopy(src, buf.at[z, core], s_d.at[0], rv.at[z], dn), has_dn)
        send(rcopy(src, buf.at[z, core], ps.at[0], pr.at[z], partner))

    def line_step(t, buf, sems):
        s_u, s_d, rv, ps, pr = sems
        below, above = z - t, z + t
        lo, hi = jnp.maximum(below, 0), jnp.minimum(above, NZ - 1)
        got_lo, got_hi = below >= 0, above < NZ
        for s, got, hop, ss, dev, n in (
            (lo, got_lo, has_up, s_u, up, 2 * t - 1),
            (hi, got_hi, has_dn, s_d, dn, 2 * t),
        ):
            piece = buf.at[s, core]
            arrived(piece, rv.at[s], got)
            if t < NZ - 1:
                send(rcopy(piece, piece, ss.at[t], rv.at[s], dev), jnp.logical_and(got, hop))
            send(rcopy(piece, piece, ps.at[n], pr.at[s], partner), got)

    c_sems = (c_up, c_dn, c_rv, c_ps, c_pr)
    a_sems = (a_up, a_dn, a_rv, a_ps, a_pr)
    line_own(cache, ckv, c_sems)
    mine = pl.ds(pl.multiple_of(core * dblk, dblk), dblk)
    theirs = pl.ds(pl.multiple_of(other * dblk, dblk), dblk)
    send(rcopy(go.at[:, theirs], gx, g_s.at[0], g_r.at[0], partner))

    def quarter(r):
        return pl.ds(pl.multiple_of(r * BLOCK, BLOCK), BLOCK)

    plane = ((rx, xn), (ry, yn), (rd, dg))
    for n, (r, dev) in enumerate(plane):
        send(rcopy(go.at[quarter(r), mine], H.at[row, core], g_s.at[1 + n], g_r.at[1 + 2 * n + core], dev))

    locals_ = [
        pltpu.make_async_copy(cache, ckv.at[z, core], loc_sem.at[0]),
        pltpu.make_async_copy(go.at[quarter(row), mine], H.at[row, core], loc_sem.at[1]),
    ]
    for c in locals_:
        c.start()

    def clear(s):
        rbuf[s] = jnp.zeros(rbuf.shape[1:], BF16)
        for h in range(2):
            cbuf[h, s] = jnp.zeros(cbuf.shape[2:], BF16)

    @pl.when(z == 0)
    def _():
        lax.fori_loop(0, NZ, lambda s, c: (clear(s), c)[1], 0)

    @pl.when(z == NZ - 1)
    def _():
        lax.fori_loop(0, NZ - 1, lambda s, c: (clear(s), c)[1], 0)
        clear(NZ)

    line_step(1, ckv, c_sems)
    arrived(gx, g_r.at[0])
    for n, (r, dev) in enumerate(plane):
        send(rcopy(gx.at[quarter(r)], H.at[row, other], g_s.at[4 + n], g_r.at[1 + 2 * n + other], dev))
    own_gx = pltpu.make_async_copy(gx.at[quarter(row)], H.at[row, other], loc_sem.at[2])
    own_gx.start()
    for c in locals_:
        c.wait()
    own_gx.wait()
    for n, (r, dev) in enumerate(plane):
        for side in range(2):
            arrived(H.at[r, side], g_r.at[1 + 2 * n + side])
    own_h = pltpu.make_async_copy(H.at[z], G.at[z, :, row], loc_sem.at[3])
    own_h.start()
    for i in range(1, NZ):
        send(rcopy(H.at[zd_of[i]], G.at[z, :, row], g_s.at[6 + i], g_r.at[26 + z], line[i]))

    def plane_send(i):
        piece = G.at[zs_of[i], :, row]
        if i == 0:
            own_h.wait()
        else:
            arrived(piece, g_r.at[26 + zs_of[i]])
        send(rcopy(piece, piece, g_s.at[10 + i], g_r.at[10 + i], xn))
        send(rcopy(piece, piece, g_s.at[14 + i], g_r.at[14 + i], yn))

    def plane_pass(i):
        zs = zs_of[i]
        arrived(G.at[zs, :, rx], g_r.at[10 + i])
        send(rcopy(G.at[zs, 0, rx], G.at[zs, 0, rx], g_s.at[18 + i], g_r.at[18 + i], yn))
        arrived(G.at[zs, :, ry], g_r.at[14 + i])
        send(rcopy(G.at[zs, 1, ry], G.at[zs, 1, ry], g_s.at[22 + i], g_r.at[22 + i], xn))

    line_step(2, ckv, c_sems)
    plane_send(0)
    line_step(3, ckv, c_sems)
    for s in range(NZ):
        arrived(ckv.at[s, other], c_pr.at[s])

    causal = (lax.broadcasted_iota(jnp.int32, (BLOCK, BLOCK), 0)
              >= lax.broadcasted_iota(jnp.int32, (BLOCK, BLOCK), 1))
    blocks = tok // BLOCK

    def head_cols(h):
        return pl.ds(pl.multiple_of(h * HEAD_DIM, HEAD_DIM), HEAD_DIM)

    def listed(kv, b, cols):
        return jnp.concatenate([ckv[tz[b, j], tc[b, j], kv, :, cols] for j in range(KB)], axis=0)

    def scores_of(rows, cols, kc):
        qb = q[rows, cols]
        s1 = dot_nt(qb, kc) * INV2
        s2 = jnp.where(causal, dot_nt(qb, k[rows, cols]) * INV2, NEG)
        return s1, s2

    def fwd_head(h, c):
        cols = head_cols(h)
        for b in range(blocks):
            rows = pl.ds(b * BLOCK, BLOCK)
            s1, s2 = scores_of(rows, cols, listed(0, b, cols))
            m = jnp.maximum(jnp.max(s1, axis=1, keepdims=True), jnp.max(s2, axis=1, keepdims=True))
            e1 = jnp.exp2(s1 - m)
            e2 = jnp.exp2(s2 - m)
            total = jnp.sum(e1, axis=1, keepdims=True) + jnp.sum(e2, axis=1, keepdims=True)
            o = dot_nn(e1.astype(BF16), listed(1, b, cols)) + dot_nn(e2.astype(BF16), v[rows, cols])
            abuf[z, core, rows, cols] = (o / total).astype(BF16)
            lse[h, rows, :] = m + jnp.log2(total)
        return c

    for b in range(blocks):
        pscr[b, KB] = jnp.zeros((BLOCK, BLOCK), BF16)
        dscr[b, KB] = jnp.zeros((BLOCK, BLOCK), BF16)
    lax.fori_loop(0, wid // HEAD_DIM, fwd_head, 0)
    line_own(abuf.at[z, core], abuf, a_sems)

    tile = 256

    def ga_part(i):
        zs = zs_of[i]
        arrived(G.at[zs, 0, rd], g_r.at[18 + i])
        arrived(G.at[zs, 1, rd], g_r.at[22 + i])

        def body(n, c):
            side = n // 2
            part = n % 2
            rows = pl.ds(pl.multiple_of(part * tile, tile), tile)
            lhs = G[zs, side, pl.ds(part * 2, 2)].reshape(tile, dblk)
            for h in range(2):
                acc = dot_nn(lhs, w[:, pl.ds(h * half, half)])
                gpart[side, zs, h, rows, :] = acc.astype(BF16)
            return c

        lax.fori_loop(0, 4, body, 0)
        send(rcopy(gpart.at[other, zs], grecv.at[zs], p_s.at[i], p_r.at[i], partner))

    def gw_tile(n):
        rows = pl.ds(n * tile, tile)
        acc = None
        for s in range(NZ):
            lhs = G[s, :, :, :, rows].reshape(2 * tok, tile)
            part = dot_tn(lhs, abuf[s].reshape(2 * tok, wid))
            acc = part if acc is None else acc + part
        gw[rows, :] = acc.astype(BF16)

    def ga_sum(s, h, rows):
        return (gpart[core, s, h, rows, :].astype(F32) + grecv[s, h, rows, :].astype(F32)
                + rbuf[s, h, rows, :].astype(F32))

    def rs_step(t, h):
        zu = NZ - 1 - t + z
        go_up = jnp.logical_and(zu > z, zu < NZ)
        su = jnp.clip(zu, 0, NZ - 1)
        zl = t - (NZ - 1) + z
        go_dn = jnp.logical_and(zl >= 0, zl < z)
        sl = jnp.clip(zl, 0, NZ - 1)
        for go_, s, got, sems, dev, dst in (
            (go_up, su, has_dn, r_up, up, su),
            (go_dn, sl, has_up, r_dn, dn, jnp.where(zl == z - 1, NZ, sl)),
        ):
            arrived(rbuf.at[s, h], r_rv.at[s, h], jnp.logical_and(go_, got))

            @pl.when(go_)
            def _(s=s):
                def body(n, c):
                    rows = pl.ds(pl.multiple_of(n * BLOCK, BLOCK), BLOCK)
                    rbuf[s, h, rows, :] = ga_sum(s, h, rows).astype(BF16)
                    return c
                lax.fori_loop(0, tok // BLOCK, body, 0)

            send(rcopy(rbuf.at[s, h], rbuf.at[dst, h], sems.at[t, h], r_rv.at[dst, h], dev), go_)

    def bwd(h):
        arrived(rbuf.at[z, h], r_rv.at[z, h], has_dn)
        arrived(rbuf.at[NZ, h], r_rv.at[NZ, h], has_up)

        def total(n, c):
            rows = pl.ds(pl.multiple_of(n * BLOCK, BLOCK), BLOCK)
            ga[rows, :] = (ga_sum(z, h, rows) + rbuf[NZ, h, rows, :].astype(F32)).astype(BF16)
            return c

        lax.fori_loop(0, blocks, total, 0)

        def head(j, c):
            hd = h * (half // HEAD_DIM) + j
            cols = head_cols(hd)
            jc = head_cols(j)
            for b in range(blocks):
                rows = pl.ds(b * BLOCK, BLOCK)
                kc = listed(0, b, cols)
                s1, s2 = scores_of(rows, cols, kc)
                norm = lse[hd, rows, :]
                p1 = jnp.exp2(s1 - norm)
                p2 = jnp.exp2(s2 - norm)
                gb = ga[rows, jc]
                d1 = dot_nt(gb, listed(1, b, cols))
                d2 = dot_nt(gb, v[rows, cols])
                delta = jnp.sum(gb.astype(F32) * abuf[z, core, rows, cols].astype(F32), axis=1, keepdims=True)
                b1 = p1.astype(BF16)
                b2 = p2.astype(BF16)
                t1 = (p1 * (d1 - delta)).astype(BF16)
                t2 = (p2 * (d2 - delta)).astype(BF16)
                for n in range(KB):
                    pscr[b, n] = b1[:, n * BLOCK : (n + 1) * BLOCK]
                    dscr[b, n] = t1[:, n * BLOCK : (n + 1) * BLOCK]
                kb = k[rows, cols]
                gq[rows, cols] = ((dot_nn(t1, kc) + dot_nn(t2, kb)) * INV).astype(BF16)
                gk[rows, cols] = (dot_tn(t2, q[rows, cols]) * INV).astype(BF16)
                gv[rows, cols] = dot_tn(b2, gb).astype(BF16)
            qh = q[:, cols]
            gh = ga[:, jc]
            for s in range(NZ):
                for side in range(2):
                    ds = jnp.concatenate([dscr[b, slot_of[b, 2 * s + side]] for b in range(blocks)], axis=0)
                    ps = jnp.concatenate([pscr[b, slot_of[b, 2 * s + side]] for b in range(blocks)], axis=0)
                    cpart[h, side, s, 0, :, jc] = (dot_tn(ds, qh) * INV).astype(BF16)
                    cpart[h, side, s, 1, :, jc] = dot_tn(ps, gh).astype(BF16)
            return c

        lax.fori_loop(0, half // HEAD_DIM, head, 0)
        send(rcopy(cpart.at[h, other], crecv.at[h], x_s.at[h], x_r.at[h], partner))

    def pair_sum(h):
        arrived(crecv.at[h], x_r.at[h])

    def cache_sum(h, s):
        return cpart[h, core, s].astype(F32) + crecv[h, s].astype(F32)

    def crs_step(t, h):
        zu = NZ - 1 - t + z
        go_up = jnp.logical_and(zu > z, zu < NZ)
        su = jnp.clip(zu, 0, NZ - 1)
        zl = t - (NZ - 1) + z
        go_dn = jnp.logical_and(zl >= 0, zl < z)
        sl = jnp.clip(zl, 0, NZ - 1)
        for go_, s, got, sems, dev, dst in (
            (go_up, su, has_dn, s_up, up, su),
            (go_dn, sl, has_up, s_dn, dn, jnp.where(zl == z - 1, NZ, sl)),
        ):
            arrived(cbuf.at[h, s], s_rv.at[s, h], jnp.logical_and(go_, got))

            @pl.when(go_)
            def _(s=s):
                cbuf[h, s] = (cbuf[h, s].astype(F32) + cache_sum(h, s)).astype(BF16)

            send(rcopy(cbuf.at[h, s], cbuf.at[h, dst], sems.at[t, h], s_rv.at[dst, h], dev), go_)

    def ga_swap(i):
        arrived(grecv.at[zs_of[i]], p_r.at[i])

    plane_send(1)
    plane_pass(0)
    line_step(1, abuf, a_sems)
    plane_send(2)
    plane_pass(1)
    plane_send(3)
    ga_part(1)
    ga_part(0)
    ga_swap(1)
    rs_step(0, 0)
    rs_step(0, 1)
    plane_pass(2)
    ga_part(2)
    plane_pass(3)
    ga_part(3)
    ga_swap(2)
    line_step(2, abuf, a_sems)
    rs_step(1, 0)
    rs_step(1, 1)
    ga_swap(3)
    ga_swap(0)
    line_step(3, abuf, a_sems)
    for s in range(NZ):
        arrived(abuf.at[s, other], a_pr.at[s])
    gw_tile(0)
    rs_step(2, 0)
    rs_step(2, 1)
    gw_tile(1)
    gw_tile(2)
    bwd(0)
    pair_sum(0)
    crs_step(0, 0)
    bwd(1)
    crs_step(1, 0)
    pair_sum(1)
    crs_step(0, 1)
    crs_step(2, 0)
    gw_tile(3)
    crs_step(1, 1)
    crs_step(2, 1)

    for h in range(2):
        arrived(cbuf.at[h, z], s_rv.at[z, h], has_dn)
        arrived(cbuf.at[h, NZ], s_rv.at[NZ, h], has_up)
        total = cache_sum(h, z) + cbuf[h, z].astype(F32) + cbuf[h, NZ].astype(F32)
        gck[:, pl.ds(h * half, half)] = total[0]
        gcv[:, pl.ds(h * half, half)] = total[1]

    for copy, cond in pending:
        when(cond, copy.wait_send)


def per_device_fused(grad_out, proj_weight, queries, keys, values, cache_keys, cache_values, block_table):
    tok, wid = queries.shape
    half = wid // 2
    dblk = proj_weight.shape[0]
    blocks = tok // BLOCK
    cache = jnp.stack([cache_keys, cache_values])
    match = block_table[:, :, None] == jnp.arange(CB, dtype=jnp.int32)
    slot_of = KB - jnp.sum(match * (KB - jnp.arange(KB, dtype=jnp.int32))[None, :, None], axis=1)
    sm = pl.BlockSpec(memory_space=pltpu.SMEM)
    vm = pl.BlockSpec(memory_space=pltpu.VMEM)
    hbm = pl.BlockSpec(memory_space=pl.ANY)
    dma = pltpu.SemaphoreType.DMA
    out = pl.pallas_call(
        fused_kernel,
        out_shape=(
            jax.ShapeDtypeStruct((tok, wid), BF16),
            jax.ShapeDtypeStruct((tok, wid), BF16),
            jax.ShapeDtypeStruct((tok, wid), BF16),
            jax.ShapeDtypeStruct((BLOCK, wid), F32),
            jax.ShapeDtypeStruct((BLOCK, wid), F32),
            jax.ShapeDtypeStruct((dblk, wid), BF16),
            jax.ShapeDtypeStruct((NZ, 2, BLOCK, dblk), BF16),
            jax.ShapeDtypeStruct((tok, dblk), BF16),
        ),
        in_specs=[hbm, vm, hbm, vm, vm, vm, sm, sm, sm],
        out_specs=[vm] * 6 + [hbm] * 2,
        scratch_shapes=[
            pltpu.VMEM((NZ, 2, 4, BLOCK, dblk), BF16),
            pltpu.VMEM((NZ, 2, 2, BLOCK, wid), BF16),
            pltpu.VMEM((NZ, 2, tok, wid), BF16),
            pltpu.VMEM((2, NZ, 2, tok, half), BF16),
            pltpu.VMEM((NZ, 2, tok, half), BF16),
            pltpu.VMEM((tok, half), BF16),
            pltpu.VMEM((NZ + 1, 2, tok, half), BF16),
            pltpu.VMEM((2, 2, NZ, 2, BLOCK, half), BF16),
            pltpu.VMEM((2, NZ, 2, BLOCK, half), BF16),
            pltpu.VMEM((2, NZ + 1, 2, BLOCK, half), BF16),
            pltpu.VMEM((blocks, KB + 1, BLOCK, BLOCK), BF16),
            pltpu.VMEM((blocks, KB + 1, BLOCK, BLOCK), BF16),
            pltpu.VMEM((wid // HEAD_DIM, tok, 1), F32),
            dma((4,)),
            dma((3,)), dma((3,)), dma((NZ,)), dma((7,)), dma((NZ,)),
            dma((3,)), dma((3,)), dma((NZ,)), dma((7,)), dma((NZ,)),
            dma((26,)), dma((26 + NZ,)),
            dma((NZ,)), dma((NZ,)),
            dma((2,)), dma((2,)),
            dma((3, 2)), dma((3, 2)), dma((NZ + 1, 2)),
            dma((3, 2)), dma((3, 2)), dma((NZ + 1, 2)),
        ],
        compiler_params=pltpu.CompilerParams(
            collective_id=0, has_side_effects=True, vmem_limit_bytes=64 * 1024 * 1024
        ),
        name="fused",
    )(grad_out, proj_weight, cache, queries, keys, values, block_table // 2, block_table % 2, slot_of)
    return out[:6]


def fits_fused(mesh):
    return mesh.shape["row"] == 4 and mesh.shape["col"] == 2 * NZ


def solution(mesh):
    in_specs = (
        P("col", "row"),
        P("col", "row"),
        P("col", "row"),
        P("col", "row"),
        P("col", "row"),
        P("col", "row"),
        P("col", "row"),
        P("col", None),
    )
    out_specs = (
        P("col", "row"),
        P("col", "row"),
        P("col", "row"),
        P("col", "row"),
        P("col", "row"),
        P("col", "row"),
    )
    return jax.shard_map(
        per_device_fused if fits_fused(mesh) else per_device, mesh=mesh, in_specs=in_specs, out_specs=out_specs, check_vma=False
    )
```
